32 devices in a mesh: fsdp: 32 (over z, y, x, core).
Axes of the slice: x: 2, y: 2, z: 4, core: 2. Of those that a mesh axis runs over, the one named last changes fastest.
Arguments:
- x_vit: bfloat16 [18432, 1024], P('fsdp'), may hold values from -6 to 6
- x_hires: bfloat16 [32768, 1536], P('fsdp'), may hold values from -6 to 6
- image_live: int32 [32], P('fsdp'), may hold values 0 or 1
- grad_vit: bfloat16 [18432, 1024], P('fsdp'), may hold values from -6 to 6
- grad_hires: bfloat16 [32768, 1536], P('fsdp'), may hold values from -6 to 6
- gain_one: bfloat16 [1024], P('fsdp'), may hold values from 0.25 to 1.75
- w_qkv: bfloat16 [1024, 3072], P('fsdp'), may hold values from -0.1875 to 0.1875
- w_out: bfloat16 [1024, 1024], P('fsdp'), may hold values from -1.5 to 1.5
- gain_two: bfloat16 [1024], P('fsdp'), may hold values from 0.25 to 1.75
- w_up: bfloat16 [1024, 4096], P('fsdp'), may hold values from -0.1875 to 0.1875
- w_down: bfloat16 [4096, 1024], P('fsdp'), may hold values from -0.1875 to 0.1875
- conv_seven: bfloat16 [49, 1536], P(None, 'fsdp'), may hold values from -0.875 to 0.875
- gain_three: bfloat16 [1536], P('fsdp'), may hold values from 0.25 to 1.75
- w_expand: bfloat16 [1536, 6144], P('fsdp'), may hold values from -0.15625 to 0.15625
- w_shrink: bfloat16 [6144, 1536], P('fsdp'), may hold values from -0.15625 to 0.15625
- layer_scale: bfloat16 [1536], P('fsdp'), may hold values from 0.29882812 to 1.5
- w_adapt: bfloat16 [1536, 1024], P('fsdp'), may hold values from -0.3125 to 0.3125
- conv_three: bfloat16 [9, 1024], P(None, 'fsdp'), may hold values from -2 to 2
- w_gate_in: bfloat16 [1024, 1024], P('fsdp'), may hold values from -0.1875 to 0.1875
- w_gate_out: bfloat16 [1024, 1024], P('fsdp'), may hold values from -0.25 to 0.25
Outputs:
- joined: bfloat16 [18432, 1024], P('fsdp')
- hires_next: bfloat16 [32768, 1536], P('fsdp')
- grad_x_vit: float32 [18432, 1024], P('fsdp')
- grad_x_hires: float32 [32768, 1536], P('fsdp')
- grad_gain_one: float32 [1024], P('fsdp')
- grad_w_qkv: float32 [1024, 3072], P('fsdp')
- grad_w_out: float32 [1024, 1024], P('fsdp')
- grad_gain_two: float32 [1024], P('fsdp')
- grad_w_up: float32 [1024, 4096], P('fsdp')
- grad_w_down: float32 [4096, 1024], P('fsdp')
- grad_conv_seven: float32 [49, 1536], P(None, 'fsdp')
- grad_gain_three: float32 [1536], P('fsdp')
- grad_w_expand: float32 [1536, 6144], P('fsdp')
- grad_w_shrink: float32 [6144, 1536], P('fsdp')
- grad_layer_scale: float32 [1536], P('fsdp')
- grad_w_adapt: float32 [1536, 1024], P('fsdp')
- grad_conv_three: float32 [9, 1024], P(None, 'fsdp')
- grad_w_gate_in: float32 [1024, 1024], P('fsdp')
- grad_w_gate_out: float32 [1024, 1024], P('fsdp')
The draws below stay inside these ranges and needn't reach their ends.
All inputs are finite; a program needn't handle non-finite values. No bound on the sum of `image_live` on one device may be relied on, other than what follows from the above.
Results may differ from the reference program's by a relative error of at most 0.02.
Values may be sent and summed in bfloat16 or wider, within the bound.
No kernel may reach another device: no remote copies, remote signals or barrier semaphores. Data moves between devices by JAX's collectives and lax.ppermute only.
A program may use at most 448 MiB of HBM per device.

```python
import math
import jax
import jax.numpy as jnp
from jax import lax

D = 1024
HEADS = 16
HEAD_DIM = 64
FF = 4096
C = 1536
CF = 6144
GH = 1024
KS = 7
KA = 3
GRID_LR = 24
GRID_HR = 32
PATCHES = 576
IMAGES = 32


def set_ends(entries, stream_key, low, largest):
    place = [jax.random.randint(jax.random.fold_in(stream_key, axis), (), 0, length) for axis, length in enumerate(entries.shape)]
    widest = entries.shape.index(max(entries.shape))
    neighbour = place[:widest] + [(place[widest] + 1) % entries.shape[widest]] + place[widest + 1:]
    return entries.at[tuple(place)].set(low).at[tuple(neighbour)].set(largest)


def raised(values, key, source, target, shards_of, factor):
    owner, partner = [(jnp.arange(values.shape[position]) // (values.shape[position] // shards_of)).reshape([-1 if axis == position else 1 for axis in range(values.ndim)]) for position in (source, target)]
    chosen = jax.random.permutation(key, shards_of)[partner]
    strong = (owner == chosen) | (owner == (partner + shards_of // 2) % shards_of)
    return jnp.where(strong, factor * values, values)


def shard_levels(rng, dims, cuts, smallest, top_value):
    def one(axis_at, blocks):
        heights = jax.random.uniform(jax.random.fold_in(jax.random.fold_in(rng, 6), axis_at), (blocks,), jnp.float32, smallest / len(cuts), top_value / len(cuts))
        return jnp.repeat(jnp.exp(heights), dims[axis_at] // blocks).reshape((-1,) + (1,) * (len(dims) - axis_at - 1))

    gain = one(*cuts[0])
    for cut in cuts[1:]:
        gain = gain * one(*cut)
    return gain


def bell_draw(rng, shape, scale, bound, pieces=(), kind=jnp.bfloat16):
    drawn = jax.random.normal(rng, shape, jnp.float32) * scale
    if len(pieces) > 0:
        drawn = shard_levels(rng, shape, pieces, -0.22, 0.18) * drawn
    return jnp.clip(drawn, min=-bound, max=bound).astype(kind)


def gaussian_with(key, shape, deviation, bound, cuts, heavy, held_as=jnp.bfloat16):
    entries = deviation * jax.random.normal(key, shape, jnp.float32)
    if cuts:
        entries = entries * shard_levels(key, shape, cuts, -0.22, 0.18)
    return jnp.clip(raised(entries, jax.random.fold_in(key, 3), *heavy), -bound, bound).astype(held_as)


def setup_inputs(seed: int = 0) -> dict:
    arg_keys = jax.random.split(jax.random.key(seed), 21)
    return {
        "x_vit": bell_draw(arg_keys[0], (IMAGES * PATCHES, D), 1.0, 6.0, ((0, 32),)),
        "x_hires": bell_draw(arg_keys[1], (IMAGES * GRID_HR * GRID_HR, C), 1.0, 6.0, ((0, 32),)),
        "image_live": set_ends((jax.random.randint(arg_keys[2], (IMAGES,), 0, 8) < 7).astype(jnp.int32), jax.random.fold_in(arg_keys[2], 1), 0, 1),
        "grad_vit": gaussian_with(arg_keys[3], (IMAGES * PATCHES, D), 1.0, 6.0, ((0, 32),), (0, 1, 32, 2.75)),
        "grad_hires": gaussian_with(arg_keys[4], (IMAGES * GRID_HR * GRID_HR, C), 1.0, 6.0, ((0, 32),), (0, 1, 32, 2.75)),
        "gain_one": jnp.clip(1.0 + 0.15 * jax.random.normal(arg_keys[5], (D,), jnp.float32), 0.25, 1.75).astype(jnp.bfloat16),
        "w_qkv": bell_draw(arg_keys[6], (D, 3 * D), D ** -0.5, 0.1875, ((0, 32),)),
        "w_out": bell_draw(arg_keys[7], (D, D), (D // 64) ** -0.5, 1.5, ((0, 32),)),
        "gain_two": jnp.clip(1.0 + 0.15 * jax.random.normal(arg_keys[8], (D,), jnp.float32), 0.25, 1.75).astype(jnp.bfloat16),
        "w_up": bell_draw(arg_keys[9], (D, FF), D ** -0.5, 0.1875, ((0, 32),)),
        "w_down": bell_draw(arg_keys[10], (FF, D), (FF // 4) ** -0.5, 0.1875, ((0, 32),)),
        "conv_seven": bell_draw(arg_keys[11], (KS * KS, C), (KS * KS) ** -0.5, 0.875, ((1, 32),)),
        "gain_three": jnp.clip(1.0 + 0.15 * jax.random.normal(arg_keys[12], (C,), jnp.float32), 0.25, 1.75).astype(jnp.bfloat16),
        "w_expand": bell_draw(arg_keys[13], (C, CF), C ** -0.5, 0.15625, ((0, 32),)),
        "w_shrink": bell_draw(arg_keys[14], (CF, C), (CF // 4) ** -0.5, 0.15625, ((0, 32),)),
        "layer_scale": jnp.clip(jnp.exp(math.log(1.5) - 1.6133518 * jax.random.uniform(arg_keys[15], (C,), jnp.float32) ** shard_levels(arg_keys[15], (C,), ((0, 32),), -0.2, 0.2)), 0.29882812, 1.5).astype(jnp.bfloat16),
        "w_adapt": bell_draw(arg_keys[16], (C, D), (C // 4) ** -0.5, 0.3125, ((0, 32),)),
        "conv_three": bell_draw(arg_keys[17], (KA * KA, D), (KA * KA) ** -0.5, 2.0, ((1, 32),)),
        "w_gate_in": bell_draw(arg_keys[18], (D, GH), D ** -0.5, 0.1875, ((0, 32),)),
        "w_gate_out": bell_draw(arg_keys[19], (GH, D), (GH // 2) ** -0.5, 0.25, ((0, 32),)),
    }


@jax.custom_vjp
def low(v):
    return lax.optimization_barrier(v.astype(jnp.bfloat16)).astype(jnp.float32)

@jax.custom_vjp
def low_back(v):
    return v

def low_keep(v):
    return (low(v), None)

def low_pass(kept, grad):
    return (grad,)

def back_keep(v):
    return (v, None)

def back_low(kept, grad):
    return (low(grad),)
low.defvjp(low_keep, low_pass)
low_back.defvjp(back_keep, back_low)

def matmul(operand, weight):
    return jnp.einsum('...i,ij->...j', operand, weight, precision=lax.Precision.HIGHEST)

def norm_rows(values, epsilon):
    average = lax.optimization_barrier(jnp.mean(values, axis=-1, keepdims=True))
    centred = values - average
    spread = lax.optimization_barrier(jnp.mean(centred * centred, axis=-1, keepdims=True))
    return centred * lax.rsqrt(spread + epsilon)

def gelu_exact(values):
    return jax.nn.gelu(values, approximate=False)

def pool_table(fine_cells, coarse_cells):
    coarse_index = jnp.arange(coarse_cells, dtype=jnp.int32)[:, None]
    fine_index = jnp.arange(fine_cells, dtype=jnp.int32)[None, :]
    window_start = coarse_index * fine_cells // coarse_cells
    window_end = ((coarse_index + 1) * fine_cells + coarse_cells - 1) // coarse_cells
    inside = ((fine_index >= window_start) & (fine_index < window_end)).astype(jnp.float32)
    return inside / lax.optimization_barrier(jnp.sum(inside, axis=1, keepdims=True))

def depthwise(grid_field, tap_weights, kernel_width):
    tap_reach = kernel_width // 2
    edge_cells = grid_field.shape[1]
    padded = jnp.pad(grid_field, ((0, 0), (tap_reach, tap_reach), (tap_reach, tap_reach), (0, 0)))
    summed = jnp.zeros_like(grid_field)
    for tap_row in range(kernel_width):
        for tap_col in range(kernel_width):
            summed = summed + padded[:, tap_row:tap_row + edge_cells, tap_col:tap_col + edge_cells] * tap_weights[tap_row * kernel_width + tap_col]
    return summed

def image_forward(weight_set, patches, hires, alive):
    gain_one, w_qkv, w_out, gain_two, w_up, w_down, conv_seven, gain_three, w_expand, w_shrink, layer_scale, w_adapt, conv_three, w_gate_in, w_gate_out = weight_set
    normed_one = low(norm_rows(patches, 1e-05) * gain_one)
    projected = low(low_back(matmul(normed_one, w_qkv)))
    queries = projected[:, :D].reshape(PATCHES, HEADS, HEAD_DIM)
    keys_part = projected[:, D:2 * D].reshape(PATCHES, HEADS, HEAD_DIM)
    values_part = projected[:, 2 * D:].reshape(PATCHES, HEADS, HEAD_DIM)
    scores = low_back(jnp.einsum('phe,khe->hpk', queries, keys_part, precision=lax.Precision.HIGHEST) * HEAD_DIM ** (-0.5))
    probs = low(jax.nn.softmax(scores, axis=-1))
    attended = jnp.einsum('hpk,khe->phe', probs, values_part, precision=lax.Precision.HIGHEST).reshape(PATCHES, D)
    attended = low(low_back(attended))
    resid_one = patches + low_back(matmul(attended, w_out))
    normed_two = low(norm_rows(resid_one, 1e-05) * gain_two)
    hidden_up = low_back(matmul(normed_two, w_up))
    resid_two = resid_one + low_back(matmul(low(gelu_exact(hidden_up)), w_down))
    conved = depthwise(hires[None], conv_seven, KS)[0]
    normed_three = low(norm_rows(conved, 1e-06) * gain_three)
    expanded = low_back(matmul(normed_three, w_expand))
    shrunk = low_back(matmul(low(gelu_exact(expanded)), w_shrink))
    hires_out = hires + layer_scale * shrunk
    table = pool_table(GRID_HR, GRID_LR)
    pooled_rows = jnp.einsum('ia,abc->ibc', table, hires_out, precision=lax.Precision.HIGHEST)
    pooled = jnp.einsum('jb,ibc->ijc', table, pooled_rows, precision=lax.Precision.HIGHEST)
    adapted = low_back(matmul(low(pooled), w_adapt))
    mixed = depthwise(adapted[None], conv_three, KA)[0].reshape(PATCHES, D)
    gate_hidden = low_back(matmul(low(mixed), w_gate_in))
    gate_value = jnp.tanh(low_back(matmul(low(gelu_exact(gate_hidden)), w_gate_out)))
    joined = alive * (resid_two + gate_value * mixed)
    return (joined, alive * hires_out)

def reference(x_vit, x_hires, image_live, grad_vit, grad_hires, gain_one, w_qkv, w_out, gain_two, w_up, w_down, conv_seven, gain_three, w_expand, w_shrink, layer_scale, w_adapt, conv_three, w_gate_in, w_gate_out):
    weight_set = tuple((weight_arg.astype(jnp.float32) for weight_arg in (gain_one, w_qkv, w_out, gain_two, w_up, w_down, conv_seven, gain_three, w_expand, w_shrink, layer_scale, w_adapt, conv_three, w_gate_in, w_gate_out)))
    patches = x_vit.astype(jnp.float32).reshape(IMAGES, PATCHES, D)
    hires = x_hires.astype(jnp.float32).reshape(IMAGES, GRID_HR, GRID_HR, C)
    alive = image_live.astype(jnp.float32)
    cot_vit = grad_vit.astype(jnp.float32).reshape(IMAGES, PATCHES, D)
    cot_hires = grad_hires.astype(jnp.float32).reshape(IMAGES, GRID_HR, GRID_HR, C)

    def one_image(totals, scan_item):
        patch_item, hires_item, alive_item, cot_first, cot_second = scan_item

        def forward(weights_in, patch_in, hires_in):
            return image_forward(weights_in, patch_in, hires_in, alive_item)
        results, pullback = jax.vjp(forward, weight_set, patch_item, hires_item)
        grad_weights, grad_patch, grad_field = pullback((cot_first, cot_second))
        totals = jax.tree.map(jnp.add, totals, grad_weights)
        return (totals, (results[0], results[1], grad_patch, grad_field))
    zero_grads = jax.tree.map(jnp.zeros_like, weight_set)
    totals, (joined, hires_next, grad_patches, grad_fields) = lax.scan(one_image, zero_grads, (patches, hires, alive, cot_vit, cot_hires))
    return (joined.reshape(IMAGES * PATCHES, D).astype(jnp.bfloat16), hires_next.reshape(IMAGES * GRID_HR * GRID_HR, C).astype(jnp.bfloat16), grad_patches.reshape(IMAGES * PATCHES, D), grad_fields.reshape(IMAGES * GRID_HR * GRID_HR, C), totals[0], totals[1], totals[2], totals[3], totals[4], totals[5], totals[6], totals[7], totals[8], totals[9], totals[10], totals[11], totals[12], totals[13], totals[14])
```

```python
import functools
import math

import jax
import jax.numpy as jnp
from jax import lax
from jax.experimental import pallas as pl
from jax.experimental.pallas import tpu as pltpu
from jax.sharding import PartitionSpec as P

D = 1024
HEAD_DIM = 64
C = 1536
KS = 7
KA = 3
GRID_LR = 24
GRID_HR = 32
LANES = 128
GROUP = 8
NN = ((1,), (0,))
NT = ((1,), (1,))
TN = ((0,), (0,))
BF16 = jnp.bfloat16
F32 = jnp.float32


def dot(left, right, dims):
    return lax.dot_general(left, right, (dims, ((), ())), preferred_element_type=F32)


def kernel_limits(mebibytes):
    return pltpu.CompilerParams(vmem_limit_bytes=mebibytes * 2**20)


def estimate(flops, moved):
    return pl.CostEstimate(flops=flops, bytes_accessed=moved, transcendentals=0)


def norm_rows(values, epsilon):
    average = jnp.mean(values, axis=-1, keepdims=True)
    centred = values - average
    spread = jnp.mean(centred * centred, axis=-1, keepdims=True)
    inverse = lax.rsqrt(spread + epsilon)
    return (centred * inverse, inverse)


def norm_back(grad_normed, normed, inverse):
    first_mean = jnp.mean(grad_normed, axis=-1, keepdims=True)
    second_mean = jnp.mean(grad_normed * normed, axis=-1, keepdims=True)
    return inverse * (grad_normed - first_mean - normed * second_mean)


def gelu_pair(values):
    cdf = 0.5 * (1.0 + lax.erf(values * (1.0 / math.sqrt(2.0))))
    density = jnp.exp(-0.5 * values * values) * (1.0 / math.sqrt(2.0 * math.pi))
    return (values * cdf, cdf + values * density)


def pool_table(fine_cells, coarse_cells):
    coarse_index = jnp.arange(coarse_cells, dtype=jnp.int32)[:, None]
    fine_index = jnp.arange(fine_cells, dtype=jnp.int32)[None, :]
    window_start = coarse_index * fine_cells // coarse_cells
    window_end = ((coarse_index + 1) * fine_cells + coarse_cells - 1) // coarse_cells
    inside = ((fine_index >= window_start) & (fine_index < window_end)).astype(jnp.float32)
    return inside / jnp.sum(inside, axis=1, keepdims=True)


def fill_shifted(shifted, field, width, edge):
    reach = width // 2
    cells, lanes = field.shape
    column = lax.broadcasted_iota(jnp.int32, (cells, lanes), 0) % edge
    for step in range(width):
        offset = step - reach
        moved = field
        if offset != 0:
            moved = pltpu.roll(field, (-offset) % cells, 0)
            inside = (column + offset >= 0) & (column + offset < edge)
            moved = jnp.where(inside, moved, 0.0)
        shifted[step, reach : reach + edge] = moved.reshape(edge, edge, lanes)


def clear_edges(shifted, width, edge):
    reach = width // 2
    border = jnp.zeros((width, reach) + shifted.shape[2:], F32)
    shifted[:, 0:reach] = border
    shifted[:, reach + edge :] = border


def depthwise_kernel(width, edge, field_ref, taps_ref, out_ref, shifted, wide):
    @pl.when(pl.program_id(0) == 0)
    def _():
        clear_edges(shifted, width, edge)

    fill_shifted(shifted, field_ref[...].astype(F32), width, edge)
    wide[...] = jnp.broadcast_to(taps_ref[...].astype(F32)[:, None, :], wide.shape)
    strips = edge // 8

    def body(index, carry):
        base = (index // strips) * GROUP
        column = pl.multiple_of((index % strips) * 8, 8)
        sums = [jnp.zeros((8, LANES), F32)] * GROUP
        for step in range(width):
            taps = [wide[tap * width + step] for tap in range(width)]
            for row in range(GROUP + width - 1):
                value = shifted[step, base + row, pl.ds(column, 8), :]
                for place in range(GROUP):
                    if 0 <= row - place < width:
                        sums[place] = sums[place] + value * taps[row - place]
        for place in range(GROUP):
            start = pl.multiple_of((base + place) * edge + column, 8)
            out_ref[pl.ds(start, 8), :] = sums[place]
        return carry

    lax.fori_loop(0, (edge // GROUP) * strips, body, 0)


def depthwise(field, taps, width, edge):
    cells, channels = field.shape
    return pl.pallas_call(
        functools.partial(depthwise_kernel, width, edge),
        grid=(channels // LANES,),
        in_specs=[
            pl.BlockSpec((cells, LANES), lambda i: (0, i)),
            pl.BlockSpec((width * width, LANES), lambda i: (0, i)),
        ],
        out_specs=pl.BlockSpec((cells, LANES), lambda i: (0, i)),
        out_shape=jax.ShapeDtypeStruct((cells, channels), F32),
        scratch_shapes=[
            pltpu.VMEM((width, edge + width - 1, edge, LANES), F32),
            pltpu.VMEM((width * width, 8, LANES), F32),
        ],
        compiler_params=kernel_limits(32),
        cost_estimate=estimate(600 * width * width * cells * channels, 8 * cells * channels),
        name="depthwise",
    )(field, taps)


def depthwise_back_kernel(
    width, edge, grad_ref, field_ref, base_ref, taps_ref, out_ref, tap_out_ref, shifted, wide, cells_ref, sums_ref
):
    @pl.when(pl.program_id(0) == 0)
    def _():
        clear_edges(shifted, width, edge)

    fill_shifted(shifted, grad_ref[...], width, edge)
    cells_ref[...] = field_ref[...].astype(F32)
    sums_ref[...] = base_ref[...]
    wide[...] = jnp.broadcast_to(taps_ref[...].astype(F32)[:, None, :], wide.shape)
    strips = edge // 8
    last = width - 1

    for step in range(width):
        taps = [wide[(last - tap) * width + (last - step)] for tap in range(width)]

        def body(index, tap_sums):
            tap_sums = list(tap_sums)
            base = (index // strips) * GROUP
            column = pl.multiple_of((index % strips) * 8, 8)
            spots = [
                pl.ds(pl.multiple_of((base + place) * edge + column, 8), 8)
                for place in range(GROUP)
            ]
            sums = [sums_ref[spot, :] for spot in spots]
            cells = [cells_ref[spot, :] for spot in spots]
            for row in range(GROUP + width - 1):
                value = shifted[step, base + row, pl.ds(column, 8), :]
                for place in range(GROUP):
                    tap = row - place
                    if 0 <= tap < width:
                        sums[place] = sums[place] + value * taps[tap]
                        tap_sums[tap] = tap_sums[tap] + value * cells[place]
            for place in range(GROUP):
                sums_ref[spots[place], :] = sums[place]
            return tuple(tap_sums)

        tap_sums = lax.fori_loop(
            0, (edge // GROUP) * strips, body, (jnp.zeros((8, LANES), F32),) * width
        )
        for tap in range(width):
            spot = (last - tap) * width + (last - step)
            tap_out_ref[spot : spot + 1, :] = jnp.sum(tap_sums[tap], axis=0, keepdims=True)
    out_ref[...] = sums_ref[...].astype(out_ref.dtype)


def depthwise_back(grad, field, base, taps, width, edge, out_type):
    cells, channels = field.shape
    full = pl.BlockSpec((cells, LANES), lambda i: (0, i))
    small = pl.BlockSpec((width * width, LANES), lambda i: (0, i))
    return pl.pallas_call(
        functools.partial(depthwise_back_kernel, width, edge),
        grid=(channels // LANES,),
        in_specs=[full, full, full, small],
        out_specs=[full, small],
        out_shape=[
            jax.ShapeDtypeStruct((cells, channels), out_type),
            jax.ShapeDtypeStruct((width * width, channels), F32),
        ],
        scratch_shapes=[
            pltpu.VMEM((width, edge + width - 1, edge, LANES), F32),
            pltpu.VMEM((width * width, 8, LANES), F32),
            pltpu.VMEM((cells, LANES), F32),
            pltpu.VMEM((cells, LANES), F32),
        ],
        compiler_params=kernel_limits(32),
        cost_estimate=estimate(1200 * width * width * cells * channels, 14 * cells * channels),
        name="depthwise_back",
    )(grad, field, base, taps)


def softmax_rows(query, key):
    scores = dot(query, key, NT) * HEAD_DIM ** (-0.5)
    raised = jnp.exp(scores - jnp.max(scores, axis=-1, keepdims=True))
    return raised * (1.0 / jnp.sum(raised, axis=-1, keepdims=True))


def attend_kernel(q_ref, k_ref, v_ref, out_ref):
    outs = []
    for head in range(out_ref.shape[1] // HEAD_DIM):
        lanes = slice(head * HEAD_DIM, (head + 1) * HEAD_DIM)
        probs = softmax_rows(q_ref[:, lanes], k_ref[:, lanes]).astype(BF16)
        outs.append(dot(probs, v_ref[:, lanes], NN))
    out_ref[...] = jnp.concatenate(outs, axis=1).astype(BF16)


def attend(qkv, width=256):
    rows = qkv.shape[0]
    steps = D // width

    def spec(part):
        return pl.BlockSpec((rows, width), lambda i: (0, i + part * steps))

    return pl.pallas_call(
        attend_kernel,
        grid=(steps,),
        in_specs=[spec(0), spec(1), spec(2)],
        out_specs=spec(0),
        out_shape=jax.ShapeDtypeStruct((rows, D), BF16),
        compiler_params=kernel_limits(48),
        cost_estimate=estimate(40 * rows * rows * D, 8 * rows * D),
        name="attend",
    )(qkv, qkv, qkv)


def attend_back_kernel(q_ref, k_ref, v_ref, g_ref, dq_ref, dk_ref, dv_ref):
    scale = HEAD_DIM ** (-0.5)
    dqs, dks, dvs = ([], [], [])
    for head in range(dq_ref.shape[1] // HEAD_DIM):
        lanes = slice(head * HEAD_DIM, (head + 1) * HEAD_DIM)
        query, key, value, grad = (q_ref[:, lanes], k_ref[:, lanes], v_ref[:, lanes], g_ref[:, lanes])
        probs = softmax_rows(query, key)
        grad_probs = dot(grad, value, NT)
        dvs.append(dot(probs.astype(BF16), grad, TN))
        total = jnp.sum(probs * grad_probs, axis=-1, keepdims=True)
        low = (probs * (grad_probs - total)).astype(BF16)
        dqs.append(dot(low, key, NN) * scale)
        dks.append(dot(low, query, TN) * scale)
    dq_ref[...] = jnp.concatenate(dqs, axis=1).astype(BF16)
    dk_ref[...] = jnp.concatenate(dks, axis=1).astype(BF16)
    dv_ref[...] = jnp.concatenate(dvs, axis=1).astype(BF16)


def attend_back(qkv, grad, width=256):
    rows = qkv.shape[0]
    steps = D // width

    def spec(part):
        return pl.BlockSpec((rows, width), lambda i: (0, i + part * steps))

    return pl.pallas_call(
        attend_back_kernel,
        grid=(steps,),
        in_specs=[spec(0), spec(1), spec(2), spec(0)],
        out_specs=[spec(0)] * 3,
        out_shape=[jax.ShapeDtypeStruct((rows, D), BF16)] * 3,
        compiler_params=kernel_limits(48),
        cost_estimate=estimate(70 * rows * rows * D, 14 * rows * D),
        name="attend_back",
    )(qkv, qkv, qkv, grad)


def mlp_both_kernel(g_ref, h_ref, wi_ref, wo_ref, out_ref, dh_ref, dwi_ref, dwo_ref):
    @pl.when(pl.program_id(0) == 0)
    def _():
        out_ref[...] = jnp.zeros_like(out_ref)
        dh_ref[...] = jnp.zeros_like(dh_ref)

    hidden = dot(h_ref[...], wi_ref[...], NN)
    back = dot(g_ref[...], wo_ref[...], NT)
    act, slope = gelu_pair(hidden)
    act = act.astype(BF16)
    out_ref[...] += dot(act, wo_ref[...], NN)
    low = (back * slope).astype(BF16)
    dh_ref[...] += dot(low, wi_ref[...], NT)
    dwi_ref[...] = dot(h_ref[...], low, TN).astype(BF16)
    dwo_ref[...] = dot(act, g_ref[...], TN).astype(BF16)


def mlp_both(grad, field, w_in, w_out, tile):
    rows, wide = field.shape
    hidden = w_out.shape[0]
    whole = pl.BlockSpec((rows, wide), lambda i: (0, 0))
    columns = pl.BlockSpec((wide, tile), lambda i: (0, i))
    lines = pl.BlockSpec((tile, wide), lambda i: (i, 0))
    return pl.pallas_call(
        mlp_both_kernel,
        grid=(hidden // tile,),
        in_specs=[whole, whole, columns, lines],
        out_specs=[whole, whole, columns, lines],
        out_shape=[
            jax.ShapeDtypeStruct((rows, wide), F32),
            jax.ShapeDtypeStruct((rows, wide), F32),
            jax.ShapeDtypeStruct((wide, hidden), BF16),
            jax.ShapeDtypeStruct((hidden, wide), BF16),
        ],
        compiler_params=kernel_limits(60),
        cost_estimate=estimate(12 * rows * wide * hidden, 8 * wide * hidden),
        name="mlp_both",
    )(grad, field, w_in, w_out)


def mlp_forward_kernel(rows, h_ref, wi_ref, wo_ref, act_ref, slope_ref, out_ref):
    @pl.when(pl.program_id(0) == 0)
    def _():
        out_ref[...] = jnp.zeros_like(out_ref)

    def body(index, carry):
        spot = pl.ds(pl.multiple_of(index * rows, rows), rows)
        act, slope = gelu_pair(dot(h_ref[spot, :], wi_ref[...], NN))
        act = act.astype(BF16)
        act_ref[spot, :] = act
        slope_ref[spot, :] = slope.astype(BF16)
        out_ref[spot, :] += dot(act, wo_ref[...], NN)
        return carry

    lax.fori_loop(0, h_ref.shape[0] // rows, body, 0)


def mlp_forward(field, w_in, w_out, tile, step):
    rows, wide = field.shape
    hidden = w_out.shape[0]
    whole = pl.BlockSpec((rows, wide), lambda i: (0, 0))
    tiles = pl.BlockSpec((rows, tile), lambda i: (0, i))
    return pl.pallas_call(
        functools.partial(mlp_forward_kernel, step),
        grid=(hidden // tile,),
        in_specs=[
            whole,
            pl.BlockSpec((wide, tile), lambda i: (0, i)),
            pl.BlockSpec((tile, wide), lambda i: (i, 0)),
        ],
        out_specs=[tiles, tiles, whole],
        out_shape=[
            jax.ShapeDtypeStruct((rows, hidden), BF16),
            jax.ShapeDtypeStruct((rows, hidden), BF16),
            jax.ShapeDtypeStruct((rows, wide), F32),
        ],
        compiler_params=kernel_limits(60),
        cost_estimate=estimate(6 * rows * wide * hidden, 4 * wide * hidden + 4 * rows * hidden),
        name="mlp_forward",
    )(field, w_in, w_out)


def outer_kernel(left_ref, right_ref, out_ref):
    out_ref[...] = dot(left_ref[...], right_ref[...], TN).astype(BF16)


def outer_sum(left, right, tile):
    rows, lines = left.shape
    columns = right.shape[1]
    return pl.pallas_call(
        outer_kernel,
        grid=(lines // tile,),
        in_specs=[
            pl.BlockSpec((rows, tile), lambda i: (0, i)),
            pl.BlockSpec((rows, columns), lambda i: (0, 0)),
        ],
        out_specs=pl.BlockSpec((tile, columns), lambda i: (i, 0)),
        out_shape=jax.ShapeDtypeStruct((lines, columns), BF16),
        compiler_params=kernel_limits(48),
        cost_estimate=estimate(3 * rows * lines * columns, 2 * lines * columns),
        name="outer_sum",
    )(left, right)


def mlp_back_kernel(step, g_ref, h_ref, slope_ref, wi_ref, wo_ref, start_ref, dh_ref, dwi_ref, low_ref):
    @pl.when(pl.program_id(0) == 0)
    def _():
        dh_ref[...] = start_ref[...]

    def body(index, carry):
        spot = pl.ds(pl.multiple_of(index * step, step), step)
        back = dot(g_ref[spot, :], wo_ref[...], NT)
        low = (back * slope_ref[spot, :].astype(F32)).astype(BF16)
        low_ref[spot, :] = low
        dh_ref[spot, :] += dot(low, wi_ref[...], NT)
        return carry

    lax.fori_loop(0, h_ref.shape[0] // step, body, 0)
    block = 256

    def outer(index, carry):
        spot = pl.ds(pl.multiple_of(index * block, block), block)
        dwi_ref[spot, :] = dot(h_ref[:, spot], low_ref[...], TN).astype(BF16)
        return carry

    lax.fori_loop(0, dwi_ref.shape[0] // block, outer, 0)


def mlp_back(grad, field, slope, w_in, w_out, start, tile, step, first, last):
    rows, wide = field.shape
    whole = pl.BlockSpec((rows, wide), lambda i: (0, 0))
    return pl.pallas_call(
        functools.partial(mlp_back_kernel, step),
        grid=(last - first,),
        in_specs=[
            whole,
            whole,
            pl.BlockSpec((rows, tile), lambda i: (0, i + first)),
            pl.BlockSpec((wide, tile), lambda i: (0, i + first)),
            pl.BlockSpec((tile, wide), lambda i: (i + first, 0)),
            whole,
        ],
        out_specs=[whole, pl.BlockSpec((wide, tile), lambda i: (0, i))],
        out_shape=[
            jax.ShapeDtypeStruct((rows, wide), F32),
            jax.ShapeDtypeStruct((wide, (last - first) * tile), BF16),
        ],
        scratch_shapes=[pltpu.VMEM((rows, tile), BF16)],
        compiler_params=kernel_limits(60),
        cost_estimate=estimate(
            7 * rows * wide * tile * (last - first), 6 * wide * tile * (last - first)
        ),
        name="mlp_back",
    )(grad, field, slope, w_in, w_out, start)


def gate_kernel(
    mixed_ref, resid_ref, gv_ref, live_ref, wi_ref, wo_ref, joined_ref, dmix_ref, dwi_ref, dwo_ref
):
    live = live_ref[0].astype(F32)
    mixed = mixed_ref[...]
    mixed_low = mixed.astype(BF16)
    act, slope = gelu_pair(dot(mixed_low, wi_ref[...], NN))
    act = act.astype(BF16)
    gate = jnp.tanh(dot(act, wo_ref[...], NN))
    joined_ref[...] = (live * (resid_ref[...] + gate * mixed)).astype(BF16)
    grad = live * gv_ref[...].astype(F32)
    logit = (grad * mixed * (1.0 - gate * gate)).astype(BF16)
    dwo_ref[...] = dot(act, logit, TN).astype(BF16)
    low = (dot(logit, wo_ref[...], NT) * slope).astype(BF16)
    dwi_ref[...] = dot(mixed_low, low, TN).astype(BF16)
    dmix_ref[...] = grad * gate + dot(low, wi_ref[...], NT)


def gate_both(mixed, resid, grad, live, w_in, w_out):
    rows, wide = mixed.shape
    place = pl.BlockSpec(memory_space=pltpu.VMEM)
    return pl.pallas_call(
        gate_kernel,
        in_specs=[place, place, place, pl.BlockSpec(memory_space=pltpu.SMEM), place, place],
        out_specs=[place] * 4,
        out_shape=[
            jax.ShapeDtypeStruct((rows, wide), BF16),
            jax.ShapeDtypeStruct((rows, wide), F32),
            jax.ShapeDtypeStruct(w_in.shape, BF16),
            jax.ShapeDtypeStruct(w_out.shape, BF16),
        ],
        compiler_params=kernel_limits(60),
        cost_estimate=estimate(20 * rows * wide * w_in.shape[1], 30 * rows * wide),
        name="gate_both",
    )(mixed, resid, grad, live, w_in, w_out)


def bit_pairs(devices, bit):
    return [(index, index ^ (1 << bit)) for index in range(devices)]


def own_bit(bit):
    return (lax.axis_index("fsdp") >> bit) & 1


def gather_small(block, devices):
    gathered = block[None]
    for bit in range(devices.bit_length() - 1):
        other = lax.ppermute(gathered, "fsdp", bit_pairs(devices, bit))
        high = own_bit(bit) == 1
        gathered = jnp.where(
            high,
            jnp.concatenate((other, gathered), axis=0),
            jnp.concatenate((gathered, other), axis=0),
        )
    return gathered


def scatter_sum(partial, bit_order, devices, link_type=jnp.bfloat16):
    bits = devices.bit_length() - 1
    rest = partial.shape[1:]
    field = partial.astype(link_type).reshape((2,) * bits + rest)
    held = list(range(bits - 1, -1, -1))
    for bit in bit_order:
        axis = held.index(bit)
        mine = own_bit(bit)
        sent = lax.dynamic_index_in_dim(field, 1 - mine, axis, keepdims=False)
        kept = lax.dynamic_index_in_dim(field, mine, axis, keepdims=False)
        arrived = lax.ppermute(sent, "fsdp", bit_pairs(devices, bit))
        total = kept.astype(jnp.float32) + arrived.astype(jnp.float32)
        held.pop(axis)
        field = total.astype(link_type) if held else total
    return field


def scatter_orders(devices):
    bits = devices.bit_length() - 1
    if bits == 5:
        x_bits, y_bits, z_bits = (1,), (2,), (3, 4)
    else:
        span = (bits - 1 + 2) // 3
        places = tuple(range(1, bits))
        x_bits, y_bits, z_bits = places[:span], places[span : 2 * span], places[2 * span :]
    return (
        (0,) + y_bits + z_bits + x_bits,
        (0,) + x_bits + z_bits + y_bits,
        (0,) + y_bits + x_bits + z_bits,
        (0,) + x_bits + y_bits + z_bits,
    )


def scatter_weight(gradient, devices, turn):
    orders = scatter_orders(devices)
    rows, columns = gradient.shape
    split = gradient.astype(jnp.bfloat16).reshape(devices, rows // devices, columns)
    third = columns // 3 // 128 * 128
    cuts = (0, third, 2 * third, columns)
    chosen = (orders[0], orders[1], orders[2 + turn % 2])
    parts = [
        scatter_sum(split[:, :, cuts[place] : cuts[place + 1]], chosen[place], devices)
        for place in range(3)
    ]
    return jnp.concatenate(parts, axis=-1)


def after(value, *earlier):
    return lax.optimization_barrier((value,) + earlier)[0]


def shards(
    x_vit,
    x_hires,
    image_live,
    grad_vit,
    grad_hires,
    gain_one,
    w_qkv,
    w_out,
    gain_two,
    w_up,
    w_down,
    conv_seven,
    gain_three,
    w_expand,
    w_shrink,
    layer_scale,
    w_adapt,
    conv_three,
    w_gate_in,
    w_gate_out,
):
    devices = lax.axis_size("fsdp")
    edge_c, edge_d = (gain_three.shape[0], gain_one.shape[0])
    small = jnp.concatenate(
        (
            conv_seven.reshape(-1),
            gain_three,
            layer_scale,
            conv_three.reshape(-1),
            gain_one,
            gain_two,
        )
    )
    small_all = gather_small(small, devices)
    marks = [0]
    for length in (KS * KS * edge_c, edge_c, edge_c, KA * KA * edge_d, edge_d, edge_d):
        marks.append(marks[-1] + length)
    small_parts = [small_all[:, marks[place] : marks[place + 1]] for place in range(6)]
    seven_taps = small_parts[0].reshape(devices, KS * KS, edge_c).swapaxes(0, 1).reshape(KS * KS, C)
    three_taps = small_parts[3].reshape(devices, KA * KA, edge_d).swapaxes(0, 1).reshape(KA * KA, D)
    gain_c, scale_c = (small_parts[1].reshape(C).astype(F32), small_parts[2].reshape(C).astype(F32))
    gain_a, gain_b = (small_parts[4].reshape(D).astype(F32), small_parts[5].reshape(D).astype(F32))

    def gathered(block):
        return lax.all_gather(block, "fsdp", axis=0, tiled=True)

    vit_all = gathered(jnp.concatenate((w_qkv, w_out, w_gate_in, w_gate_out), axis=1))
    qkv_all = vit_all[:, : 3 * D]
    out_all = vit_all[:, 3 * D : 4 * D]
    gate_in_all = vit_all[:, 4 * D : 5 * D]
    gate_out_all = vit_all[:, 5 * D :]
    up_all = gathered(w_up)
    down_all = gathered(w_down)
    expand_all = gathered(jnp.concatenate((w_expand, w_adapt), axis=1))
    adapt_all = expand_all[:, w_expand.shape[1] :]
    shrink_all = gathered(w_shrink)

    live = image_live.astype(F32)
    grad_joined_low = (grad_vit.astype(F32) * live).astype(BF16)

    patch_in = x_vit.astype(F32)
    normed_a, inverse_a = norm_rows(patch_in, 1e-05)
    normed_a_low = (normed_a * gain_a).astype(BF16)
    qkv_low = dot(normed_a_low, qkv_all, NN).astype(BF16)
    attended_low = attend(qkv_low)
    resid_one = patch_in + dot(attended_low, out_all, NN)
    normed_b, inverse_b = norm_rows(resid_one, 1e-05)
    normed_b_low = (normed_b * gain_b).astype(BF16)
    mlp_out, grad_b, d_up, d_down = mlp_both(grad_joined_low, normed_b_low, up_all, down_all, 1024)
    resid_two = resid_one + mlp_out
    d_gain_two = jnp.sum(grad_b * normed_b, axis=0)
    grad_first = grad_joined_low.astype(F32) + norm_back(grad_b * gain_b, normed_b, inverse_b)
    grad_first_low = grad_first.astype(BF16)
    d_out = dot(attended_low, grad_first_low, TN).astype(BF16)
    grad_att_low = dot(grad_first_low, out_all, NT).astype(BF16)
    grad_qkv_low = jnp.concatenate(attend_back(qkv_low, grad_att_low), axis=1)
    d_qkv = dot(normed_a_low, grad_qkv_low, TN).astype(BF16)
    grad_a = dot(grad_qkv_low, qkv_all, NT)
    d_gain_one = jnp.sum(grad_a * normed_a, axis=0)
    grad_patches = grad_first + norm_back(grad_a * gain_a, normed_a, inverse_a)

    conved = depthwise(x_hires, seven_taps, KS, GRID_HR)
    normed_c, inverse_c = norm_rows(conved, 1e-06)
    normed_c_low = (normed_c * gain_c).astype(BF16)
    activated, slope, shrunk = mlp_forward(normed_c_low, expand_all, shrink_all, 1024, 256)
    hires_out = x_hires.astype(F32) + scale_c * shrunk
    hires_next = (live * hires_out).astype(BF16)

    table = pool_table(GRID_HR, GRID_LR)
    pool = jnp.einsum("ia,jb->ijab", table, table).reshape(GRID_LR**2, GRID_HR**2).astype(BF16)
    pooled_low = dot(pool, hires_out.astype(BF16), NN).astype(BF16)
    adapted = dot(pooled_low, adapt_all, NN)
    mixed = depthwise(adapted, three_taps, KA, GRID_LR)
    joined, grad_mixed, d_gate_in, d_gate_out = gate_both(
        mixed, resid_two, grad_vit, image_live, gate_in_all, gate_out_all
    )
    grad_adapted_low, d_conv_three = depthwise_back(
        grad_mixed, adapted, jnp.zeros_like(adapted), three_taps, KA, GRID_LR, BF16
    )
    d_adapt = dot(pooled_low, grad_adapted_low, TN).astype(BF16)
    grad_pooled_low = dot(grad_adapted_low, adapt_all, NT).astype(BF16)
    grad_hires_out = live * grad_hires.astype(F32) + dot(pool, grad_pooled_low, TN)

    d_layer_scale = jnp.sum(grad_hires_out * shrunk, axis=0)
    grad_shrunk_low = (grad_hires_out * scale_c).astype(BF16)
    d_shrink = outer_sum(activated, grad_shrunk_low, 512)
    tile = 1024
    tiles = activated.shape[1] // tile
    grad_c, d_expand = mlp_back(
        grad_shrunk_low,
        normed_c_low,
        slope,
        expand_all,
        shrink_all,
        jnp.zeros((x_hires.shape[0], C), F32),
        tile,
        256,
        0,
        tiles,
    )
    d_gain_three = jnp.sum(grad_c * normed_c, axis=0)
    grad_conved = norm_back(grad_c * gain_c, normed_c, inverse_c)
    grad_hires_in, d_conv_seven = depthwise_back(
        grad_conved, x_hires, grad_hires_out, seven_taps, KS, GRID_HR, F32
    )

    def shares(gradient):
        return gradient.reshape(devices, gradient.shape[0] // devices, gradient.shape[1])

    g_down = scatter_weight(d_down, devices, 0)
    g_up = scatter_weight(d_up, devices, 1)
    g_square = scatter_weight(
        jnp.concatenate((shares(d_out), shares(d_gate_in), shares(d_gate_out), shares(d_adapt)), axis=1).reshape(-1, D),
        devices,
        0,
    )
    g_qkv = scatter_weight(d_qkv, devices, 1)
    g_shrink = scatter_weight(d_shrink, devices, 0)
    g_expand = scatter_weight(d_expand, devices, 1)
    small_grads = jnp.concatenate(
        (
            d_conv_seven.reshape(KS * KS, devices, edge_c).swapaxes(0, 1).reshape(devices, -1),
            d_gain_three.reshape(devices, edge_c),
            d_layer_scale.reshape(devices, edge_c),
            d_conv_three.reshape(KA * KA, devices, edge_d).swapaxes(0, 1).reshape(devices, -1),
            d_gain_one.reshape(devices, edge_d),
            d_gain_two.reshape(devices, edge_d),
        ),
        axis=1,
    )
    small_sums = scatter_sum(small_grads, scatter_orders(devices)[0], devices, F32)
    small_outs = [small_sums[marks[place] : marks[place + 1]] for place in range(6)]
    return (
        joined,
        hires_next,
        grad_patches,
        grad_hires_in,
        small_outs[4],
        g_qkv,
        g_square[:edge_d],
        small_outs[5],
        g_up,
        g_down,
        small_outs[0].reshape(KS * KS, edge_c),
        small_outs[1],
        g_expand,
        g_shrink,
        small_outs[2],
        g_square[3 * edge_d :],
        small_outs[3].reshape(KA * KA, edge_d),
        g_square[edge_d : 2 * edge_d],
        g_square[2 * edge_d : 3 * edge_d],
    )


def solution(mesh):
    in_specs = (
        P("fsdp", None),
        P("fsdp", None),
        P("fsdp"),
        P("fsdp", None),
        P("fsdp", None),
        P("fsdp"),
        P("fsdp", None),
        P("fsdp", None),
        P("fsdp"),
        P("fsdp", None),
        P("fsdp", None),
        P(None, "fsdp"),
        P("fsdp"),
        P("fsdp", None),
        P("fsdp", None),
        P("fsdp"),
        P("fsdp", None),
        P(None, "fsdp"),
        P("fsdp", None),
        P("fsdp", None),
    )
    out_specs = (
        P("fsdp", None),
        P("fsdp", None),
        P("fsdp", None),
        P("fsdp", None),
        P("fsdp"),
        P("fsdp", None),
        P("fsdp", None),
        P("fsdp"),
        P("fsdp", None),
        P("fsdp", None),
        P(None, "fsdp"),
        P("fsdp"),
        P("fsdp", None),
        P("fsdp", None),
        P("fsdp"),
        P("fsdp", None),
        P(None, "fsdp"),
        P("fsdp", None),
        P("fsdp", None),
    )
    return jax.shard_map(shards, mesh=mesh, in_specs=in_specs, out_specs=out_specs, check_vma=False)
```

```python
import functools
import math

import jax
import jax.numpy as jnp
from jax import lax
from jax.experimental import pallas as pl
from jax.experimental.pallas import tpu as pltpu
from jax.sharding import PartitionSpec as P

D = 1024
HEAD_DIM = 64
C = 1536
KS = 7
KA = 3
GRID_LR = 24
GRID_HR = 32
LANES = 128
GROUP = 8
NN = ((1,), (0,))
NT = ((1,), (1,))
TN = ((0,), (0,))
BF16 = jnp.bfloat16
F32 = jnp.float32


def dot(left, right, dims):
    return lax.dot_general(left, right, (dims, ((), ())), preferred_element_type=F32)


def kernel_limits(mebibytes):
    return pltpu.CompilerParams(vmem_limit_bytes=mebibytes * 2**20)


def estimate(flops, moved):
    return pl.CostEstimate(flops=flops, bytes_accessed=moved, transcendentals=0)


def norm_rows(values, epsilon):
    average = jnp.mean(values, axis=-1, keepdims=True)
    centred = values - average
    spread = jnp.mean(centred * centred, axis=-1, keepdims=True)
    inverse = lax.rsqrt(spread + epsilon)
    return (centred * inverse, inverse)


def norm_back(grad_normed, normed, inverse):
    first_mean = jnp.mean(grad_normed, axis=-1, keepdims=True)
    second_mean = jnp.mean(grad_normed * normed, axis=-1, keepdims=True)
    return inverse * (grad_normed - first_mean - normed * second_mean)


def gelu_pair(values):
    cdf = 0.5 * (1.0 + lax.erf(values * (1.0 / math.sqrt(2.0))))
    density = jnp.exp(-0.5 * values * values) * (1.0 / math.sqrt(2.0 * math.pi))
    return (values * cdf, cdf + values * density)


def pool_table(fine_cells, coarse_cells):
    coarse_index = jnp.arange(coarse_cells, dtype=jnp.int32)[:, None]
    fine_index = jnp.arange(fine_cells, dtype=jnp.int32)[None, :]
    window_start = coarse_index * fine_cells // coarse_cells
    window_end = ((coarse_index + 1) * fine_cells + coarse_cells - 1) // coarse_cells
    inside = ((fine_index >= window_start) & (fine_index < window_end)).astype(jnp.float32)
    return inside / jnp.sum(inside, axis=1, keepdims=True)


def fill_shifted(shifted, field, width, edge):
    reach = width // 2
    cells, lanes = field.shape
    column = lax.broadcasted_iota(jnp.int32, (cells, lanes), 0) % edge
    for step in range(width):
        offset = step - reach
        moved = field
        if offset != 0:
            moved = pltpu.roll(field, (-offset) % cells, 0)
            inside = (column + offset >= 0) & (column + offset < edge)
            moved = jnp.where(inside, moved, 0.0)
        shifted[step, reach : reach + edge] = moved.reshape(edge, edge, lanes)


def clear_edges(shifted, width, edge):
    reach = width // 2
    border = jnp.zeros((width, reach) + shifted.shape[2:], F32)
    shifted[:, 0:reach] = border
    shifted[:, reach + edge :] = border


def depthwise_kernel(width, edge, field_ref, taps_ref, out_ref, shifted, wide):
    @pl.when(pl.program_id(0) == 0)
    def _():
        clear_edges(shifted, width, edge)

    fill_shifted(shifted, field_ref[...].astype(F32), width, edge)
    wide[...] = jnp.broadcast_to(taps_ref[...].astype(F32)[:, None, :], wide.shape)
    strips = edge // 8

    def body(index, carry):
        base = (index // strips) * GROUP
        column = pl.multiple_of((index % strips) * 8, 8)
        sums = [jnp.zeros((8, LANES), F32)] * GROUP
        for step in range(width):
            taps = [wide[tap * width + step] for tap in range(width)]
            for row in range(GROUP + width - 1):
                value = shifted[step, base + row, pl.ds(column, 8), :]
                for place in range(GROUP):
                    if 0 <= row - place < width:
                        sums[place] = sums[place] + value * taps[row - place]
        for place in range(GROUP):
            start = pl.multiple_of((base + place) * edge + column, 8)
            out_ref[pl.ds(start, 8), :] = sums[place]
        return carry

    lax.fori_loop(0, (edge // GROUP) * strips, body, 0)


def depthwise(field, taps, width, edge):
    cells, channels = field.shape
    return pl.pallas_call(
        functools.partial(depthwise_kernel, width, edge),
        grid=(channels // LANES,),
        in_specs=[
            pl.BlockSpec((cells, LANES), lambda i: (0, i)),
            pl.BlockSpec((width * width, LANES), lambda i: (0, i)),
        ],
        out_specs=pl.BlockSpec((cells, LANES), lambda i: (0, i)),
        out_shape=jax.ShapeDtypeStruct((cells, channels), F32),
        scratch_shapes=[
            pltpu.VMEM((width, edge + width - 1, edge, LANES), F32),
            pltpu.VMEM((width * width, 8, LANES), F32),
        ],
        compiler_params=kernel_limits(32),
        cost_estimate=estimate(600 * width * width * cells * channels, 8 * cells * channels),
        name="depthwise",
    )(field, taps)


def depthwise_back_kernel(
    width, edge, grad_ref, field_ref, base_ref, taps_ref, out_ref, tap_out_ref, shifted, wide, cells_ref, sums_ref
):
    @pl.when(pl.program_id(0) == 0)
    def _():
        clear_edges(shifted, width, edge)

    fill_shifted(shifted, grad_ref[...], width, edge)
    cells_ref[...] = field_ref[...].astype(F32)
    sums_ref[...] = base_ref[...].astype(F32)
    wide[...] = jnp.broadcast_to(taps_ref[...].astype(F32)[:, None, :], wide.shape)
    strips = edge // 8
    last = width - 1

    for step in range(width):
        taps = [wide[(last - tap) * width + (last - step)] for tap in range(width)]

        def body(index, tap_sums):
            tap_sums = list(tap_sums)
            base = (index // strips) * GROUP
            column = pl.multiple_of((index % strips) * 8, 8)
            spots = [
                pl.ds(pl.multiple_of((base + place) * edge + column, 8), 8)
                for place in range(GROUP)
            ]
            sums = [sums_ref[spot, :] for spot in spots]
            cells = [cells_ref[spot, :] for spot in spots]
            for row in range(GROUP + width - 1):
                value = shifted[step, base + row, pl.ds(column, 8), :]
                for place in range(GROUP):
                    tap = row - place
                    if 0 <= tap < width:
                        sums[place] = sums[place] + value * taps[tap]
                        tap_sums[tap] = tap_sums[tap] + value * cells[place]
            for place in range(GROUP):
                sums_ref[spots[place], :] = sums[place]
            return tuple(tap_sums)

        tap_sums = lax.fori_loop(
            0, (edge // GROUP) * strips, body, (jnp.zeros((8, LANES), F32),) * width
        )
        for tap in range(width):
            spot = (last - tap) * width + (last - step)
            tap_out_ref[spot : spot + 1, :] = jnp.sum(tap_sums[tap], axis=0, keepdims=True)
    out_ref[...] = sums_ref[...].astype(out_ref.dtype)


def depthwise_back(grad, field, base, taps, width, edge, first, last):
    cells, channels = field.shape
    skip = first // LANES
    full = pl.BlockSpec((cells, LANES), lambda i: (0, i + skip))
    small = pl.BlockSpec((width * width, LANES), lambda i: (0, i + skip))
    return pl.pallas_call(
        functools.partial(depthwise_back_kernel, width, edge),
        grid=((last - first) // LANES,),
        in_specs=[full, full, full, small],
        out_specs=[full, pl.BlockSpec((width * width, LANES), lambda i: (0, i))],
        out_shape=[
            jax.ShapeDtypeStruct((cells, channels), base.dtype),
            jax.ShapeDtypeStruct((width * width, last - first), F32),
        ],
        scratch_shapes=[
            pltpu.VMEM((width, edge + width - 1, edge, LANES), F32),
            pltpu.VMEM((width * width, 8, LANES), F32),
            pltpu.VMEM((cells, LANES), F32),
            pltpu.VMEM((cells, LANES), F32),
        ],
        input_output_aliases={2: 0},
        compiler_params=kernel_limits(32),
        cost_estimate=estimate(
            1200 * width * width * cells * (last - first), 14 * cells * (last - first)
        ),
        name="depthwise_back",
    )(grad, field, base, taps)


def softmax_rows(query, key):
    scores = dot(query, key, NT) * HEAD_DIM ** (-0.5)
    raised = jnp.exp(scores - jnp.max(scores, axis=-1, keepdims=True))
    return raised * (1.0 / jnp.sum(raised, axis=-1, keepdims=True))


def attend_kernel(q_ref, k_ref, v_ref, out_ref):
    outs = []
    for head in range(out_ref.shape[1] // HEAD_DIM):
        lanes = slice(head * HEAD_DIM, (head + 1) * HEAD_DIM)
        probs = softmax_rows(q_ref[:, lanes], k_ref[:, lanes]).astype(BF16)
        outs.append(dot(probs, v_ref[:, lanes], NN))
    out_ref[...] = jnp.concatenate(outs, axis=1).astype(BF16)


def attend(qkv, width=256):
    rows = qkv.shape[0]
    steps = D // width

    def spec(part):
        return pl.BlockSpec((rows, width), lambda i: (0, i + part * steps))

    return pl.pallas_call(
        attend_kernel,
        grid=(steps,),
        in_specs=[spec(0), spec(1), spec(2)],
        out_specs=spec(0),
        out_shape=jax.ShapeDtypeStruct((rows, D), BF16),
        compiler_params=kernel_limits(48),
        cost_estimate=estimate(40 * rows * rows * D, 8 * rows * D),
        name="attend",
    )(qkv, qkv, qkv)


def attend_back_kernel(q_ref, k_ref, v_ref, g_ref, dq_ref, dk_ref, dv_ref):
    scale = HEAD_DIM ** (-0.5)
    dqs, dks, dvs = ([], [], [])
    for head in range(dq_ref.shape[1] // HEAD_DIM):
        lanes = slice(head * HEAD_DIM, (head + 1) * HEAD_DIM)
        query, key, value, grad = (q_ref[:, lanes], k_ref[:, lanes], v_ref[:, lanes], g_ref[:, lanes])
        probs = softmax_rows(query, key)
        grad_probs = dot(grad, value, NT)
        dvs.append(dot(probs.astype(BF16), grad, TN))
        total = jnp.sum(probs * grad_probs, axis=-1, keepdims=True)
        low = (probs * (grad_probs - total)).astype(BF16)
        dqs.append(dot(low, key, NN) * scale)
        dks.append(dot(low, query, TN) * scale)
    dq_ref[...] = jnp.concatenate(dqs, axis=1).astype(BF16)
    dk_ref[...] = jnp.concatenate(dks, axis=1).astype(BF16)
    dv_ref[...] = jnp.concatenate(dvs, axis=1).astype(BF16)


def attend_back(qkv, grad, width=256):
    rows = qkv.shape[0]
    steps = D // width

    def spec(part):
        return pl.BlockSpec((rows, width), lambda i: (0, i + part * steps))

    return pl.pallas_call(
        attend_back_kernel,
        grid=(steps,),
        in_specs=[spec(0), spec(1), spec(2), spec(0)],
        out_specs=[spec(0)] * 3,
        out_shape=[jax.ShapeDtypeStruct((rows, D), BF16)] * 3,
        compiler_params=kernel_limits(48),
        cost_estimate=estimate(70 * rows * rows * D, 14 * rows * D),
        name="attend_back",
    )(qkv, qkv, qkv, grad)


def start_copies(plan, me, sources, target, semaphore, first=0, last=None):
    for source, (slots, rows, offset, begin, end) in zip(sources, plan):
        left, right = (max(begin, first), end if last is None else min(end, last))
        if left >= right:
            continue
        for place, slot in enumerate(slots):
            line = 0 if slot is None else pl.multiple_of((me ^ slot) * rows, rows)
            pltpu.make_async_copy(
                source.at[place, :, pl.ds(left - begin + offset, right - left)],
                target.at[pl.ds(line, rows), pl.ds(left - first, right - left)],
                semaphore,
            ).start()


def store_shares(value, rows, even, mine_ref, theirs_ref, lines=slice(None)):
    low = value.astype(BF16).reshape(-1, 2, rows, value.shape[-1])

    @pl.when(even)
    def _():
        mine_ref[lines] = low[:, 0]
        theirs_ref[lines] = low[:, 1]

    @pl.when(jnp.logical_not(even))
    def _():
        mine_ref[lines] = low[:, 1]
        theirs_ref[lines] = low[:, 0]


def share_type(devices, rows, columns):
    return jax.ShapeDtypeStruct((devices // 2, rows, columns), BF16)


SCALARS = pl.BlockSpec(memory_space=pltpu.SMEM)
ANYWHERE = pl.BlockSpec(memory_space=pl.ANY)
LOCAL = pl.BlockSpec(memory_space=pltpu.VMEM)


def mlp_both_kernel(shares, me_ref, g_ref, h_ref, wi_ref, wo_ref, out_ref, dh_ref, *grads):
    @pl.when(pl.program_id(0) == 0)
    def _():
        out_ref[...] = jnp.zeros_like(out_ref)
        dh_ref[...] = jnp.zeros_like(dh_ref)

    hidden = dot(h_ref[...], wi_ref[...], NN)
    back = dot(g_ref[...], wo_ref[...], NT)
    act, slope = gelu_pair(hidden)
    act = act.astype(BF16)
    out_ref[...] += dot(act, wo_ref[...], NN)
    low = (back * slope).astype(BF16)
    dh_ref[...] += dot(low, wi_ref[...], NT)
    even = me_ref[0] % 2 == 0
    if shares[0]:
        store_shares(dot(h_ref[...], low, TN), shares[0], even, *grads[:2])
    else:
        grads[0][...] = dot(h_ref[...], low, TN).astype(BF16)
    store_shares(dot(act, g_ref[...], TN), shares[1], even, *grads[-2:])


def mlp_both(grad, field, w_in, w_out, me, devices, tile):
    rows, wide = field.shape
    hidden = w_out.shape[0]
    whole = pl.BlockSpec((rows, wide), lambda i: (0, 0), pipeline_mode=pl.Buffered(1))
    total = pl.BlockSpec((rows, wide), lambda i: (0, 0))
    columns = pl.BlockSpec((wide, tile), lambda i: (0, i))
    in_rows, out_rows = (wide // devices, hidden // devices)
    in_specs = [pl.BlockSpec((devices // 2, in_rows, tile), lambda i: (0, 0, i))] * 2
    in_types = [share_type(devices, in_rows, hidden)] * 2
    if in_rows % 16:
        in_rows = 0
        in_specs = [columns]
        in_types = [jax.ShapeDtypeStruct((wide, hidden), BF16)]
    out_block = pl.BlockSpec((tile // out_rows // 2, out_rows, wide), lambda i: (i, 0, 0))
    outs = pl.pallas_call(
        functools.partial(mlp_both_kernel, (in_rows, out_rows)),
        grid=(hidden // tile,),
        in_specs=[SCALARS, whole, whole, columns, pl.BlockSpec((tile, wide), lambda i: (i, 0))],
        out_specs=[total, total] + in_specs + [out_block] * 2,
        out_shape=[
            jax.ShapeDtypeStruct((rows, wide), F32),
            jax.ShapeDtypeStruct((rows, wide), F32),
        ]
        + in_types
        + [share_type(devices, out_rows, wide)] * 2,
        compiler_params=kernel_limits(60),
        cost_estimate=estimate(14 * rows * wide * hidden, 8 * wide * hidden),
        name="mlp_both",
    )(me, grad, field, w_in, w_out)
    return (outs[0], outs[1], outs[2:-2], outs[-2:])


def mlp_forward_kernel(plan_in, plan_out, tile, tiles, rows, me_ref, h_ref, *refs):
    count = len(plan_in)
    sources_in, sources_out = (refs[:count], refs[count : count + len(plan_out)])
    act_ref, slope_ref, out_ref, wi_natural, wo_natural, wi_two, wo_all, sems = refs[
        count + len(plan_out) :
    ]
    step = pl.program_id(0)
    me = me_ref[0]

    def load(number):
        slot = number % 2
        start_copies(
            plan_in, me, sources_in, wi_two.at[slot], sems.at[slot], number * tile, (number + 1) * tile
        )

    def save(number, slot):
        return pltpu.make_async_copy(
            wi_two.at[slot],
            wi_natural.at[:, pl.ds(pl.multiple_of(number * tile, tile), tile)],
            sems.at[2 + slot],
        )

    @pl.when(step == 0)
    def _():
        load(0)
        start_copies(plan_out, me, sources_out, wo_all, sems.at[4])
        out_ref[...] = jnp.zeros_like(out_ref)

    slot = step % 2
    pltpu.make_async_copy(wi_two.at[slot], wi_two.at[slot], sems.at[slot]).wait()
    save(step, slot).start()

    @pl.when(step > 0)
    def _():
        save(step - 1, 1 - slot).wait()

    for number in range(1, tiles):

        @pl.when(step == number - 1)
        def _():
            load(number)

    @pl.when(step == 0)
    def _():
        pltpu.make_async_copy(wo_all, wo_all, sems.at[4]).wait()
        pltpu.make_async_copy(wo_all, wo_natural, sems.at[5]).start()

    @pl.when(step * tile < wo_all.shape[0])
    def _():
        def body(index, carry):
            spot = pl.ds(pl.multiple_of(index * rows, rows), rows)
            act, slope = gelu_pair(dot(h_ref[spot, :], wi_two[slot], NN))
            act = act.astype(BF16)
            act_ref[spot, :] = act
            slope_ref[spot, :] = slope.astype(BF16)
            lines = pl.ds(pl.multiple_of(step * tile, tile), tile)
            out_ref[spot, :] += dot(act, wo_all[lines, :], NN)
            return carry

        lax.fori_loop(0, h_ref.shape[0] // rows, body, 0)

    @pl.when(step == tiles - 1)
    def _():
        save(step, slot).wait()
        pltpu.make_async_copy(wo_all, wo_natural, sems.at[5]).wait()


def mlp_forward(field, pieces_in, pieces_out, me, hidden, columns, tile, step):
    plan_in, sources_in = pieces_in
    plan_out, sources_out = pieces_out
    rows, wide = field.shape
    last = hidden // tile - 1
    whole = pl.BlockSpec((rows, wide), lambda i: (0, 0), pipeline_mode=pl.Buffered(1))
    tiles = pl.BlockSpec((rows, tile), lambda i: (0, jnp.minimum(i, last)))
    anywhere = pl.BlockSpec(memory_space=pl.ANY)
    return pl.pallas_call(
        functools.partial(mlp_forward_kernel, plan_in, plan_out, tile, columns // tile, step),
        grid=(columns // tile,),
        in_specs=[pl.BlockSpec(memory_space=pltpu.SMEM), whole]
        + [anywhere] * (len(sources_in) + len(sources_out)),
        out_specs=[tiles, tiles, whole, anywhere, anywhere],
        out_shape=[
            jax.ShapeDtypeStruct((rows, hidden), BF16),
            jax.ShapeDtypeStruct((rows, hidden), BF16),
            jax.ShapeDtypeStruct((rows, wide), F32),
            jax.ShapeDtypeStruct((wide, columns), BF16),
            jax.ShapeDtypeStruct((hidden, wide), BF16),
        ],
        scratch_shapes=[
            pltpu.VMEM((2, wide, tile), BF16),
            pltpu.VMEM((hidden, wide), BF16),
            pltpu.SemaphoreType.DMA((6,)),
        ],
        compiler_params=kernel_limits(60),
        cost_estimate=estimate(7 * rows * wide * hidden, 8 * wide * hidden + 4 * rows * hidden),
        name="mlp_forward",
    )(me, field, *sources_in, *sources_out)


def outer_kernel(shares, me_ref, left_ref, right_ref, mine_ref, theirs_ref):
    value = dot(left_ref[...], right_ref[...], TN)
    store_shares(value, shares, me_ref[0] % 2 == 0, mine_ref, theirs_ref)


def outer_sum(left, right, me, share):
    rows, lines = left.shape
    columns = right.shape[1]
    tile = 4 * share if share >= 192 else 16 * share
    block = pl.BlockSpec((tile // share // 2, share, columns), lambda i: (i, 0, 0))
    return pl.pallas_call(
        functools.partial(outer_kernel, share),
        grid=(lines // tile,),
        in_specs=[
            SCALARS,
            pl.BlockSpec((rows, tile), lambda i: (0, i)),
            pl.BlockSpec((rows, columns), lambda i: (0, 0), pipeline_mode=pl.Buffered(1)),
        ],
        out_specs=[block] * 2,
        out_shape=[share_type(lines // share, share, columns)] * 2,
        compiler_params=kernel_limits(48),
        cost_estimate=estimate(3 * rows * lines * columns, 2 * lines * columns),
        name="outer_sum",
    )(me, left, right)


def mlp_back_kernel(
    step, share, me_ref, g_ref, h_ref, slope_ref, wi_ref, wo_ref, start_ref, dh_ref, *refs
):
    *grads, low_ref = refs

    @pl.when(pl.program_id(0) == 0)
    def _():
        dh_ref[...] = start_ref[...]

    def body(index, carry):
        spot = pl.ds(pl.multiple_of(index * step, step), step)
        back = dot(g_ref[spot, :], wo_ref[...], NT)
        low = (back * slope_ref[spot, :].astype(F32)).astype(BF16)
        low_ref[spot, :] = low
        dh_ref[spot, :] += dot(low, wi_ref[...], NT)
        return carry

    lax.fori_loop(0, h_ref.shape[0] // step, body, 0)
    block = 384
    even = me_ref[0] % 2 == 0

    def outer(index, carry):
        spot = pl.ds(pl.multiple_of(index * block, block), block)
        value = dot(h_ref[:, spot], low_ref[...], TN)
        if share:
            pairs = block // share // 2
            store_shares(value, share, even, *grads, pl.ds(index * pairs, pairs))
        else:
            grads[0][spot, :] = value.astype(BF16)
        return carry

    lax.fori_loop(0, h_ref.shape[1] // block, outer, 0)


def mlp_back(grad, field, slope, w_in, w_out, start, me, devices, tile, step, first, last):
    rows, wide = field.shape
    width = (last - first) * tile
    whole = pl.BlockSpec((rows, wide), lambda i: (0, 0), pipeline_mode=pl.Buffered(1))
    share = wide // devices
    grad_specs = [pl.BlockSpec((devices // 2, share, tile), lambda i: (0, 0, i))] * 2
    grad_types = [share_type(devices, share, width)] * 2
    if share % 16:
        share = 0
        grad_specs = [pl.BlockSpec((wide, tile), lambda i: (0, i))]
        grad_types = [jax.ShapeDtypeStruct((wide, width), BF16)]
    outs = pl.pallas_call(
        functools.partial(mlp_back_kernel, step, share),
        grid=(last - first,),
        in_specs=[
            SCALARS,
            whole,
            whole,
            pl.BlockSpec((rows, tile), lambda i: (0, i + first)),
            pl.BlockSpec((wide, tile), lambda i: (0, i + first)),
            pl.BlockSpec((tile, wide), lambda i: (i + first, 0)),
            whole,
        ],
        out_specs=[whole] + grad_specs,
        out_shape=[jax.ShapeDtypeStruct((rows, wide), F32)] + grad_types,
        scratch_shapes=[pltpu.VMEM((rows, tile), BF16)],
        compiler_params=kernel_limits(60),
        cost_estimate=estimate(7 * rows * wide * width, 6 * wide * width),
        name="mlp_back",
    )(me, grad, field, slope, w_in, w_out, start)
    return (outs[0], outs[1:])


def gate_kernel(
    mixed_ref, resid_ref, gv_ref, live_ref, wi_ref, wo_ref, joined_ref, dmix_ref, dwi_ref, dwo_ref
):
    live = live_ref[0].astype(F32)
    mixed = mixed_ref[...]
    mixed_low = mixed.astype(BF16)
    act, slope = gelu_pair(dot(mixed_low, wi_ref[...], NN))
    act = act.astype(BF16)
    gate = jnp.tanh(dot(act, wo_ref[...], NN))
    joined_ref[...] = (live * (resid_ref[...] + gate * mixed)).astype(BF16)
    grad = live * gv_ref[...].astype(F32)
    logit = (grad * mixed * (1.0 - gate * gate)).astype(BF16)
    dwo_ref[...] = dot(act, logit, TN).astype(BF16)
    low = (dot(logit, wo_ref[...], NT) * slope).astype(BF16)
    dwi_ref[...] = dot(mixed_low, low, TN).astype(BF16)
    dmix_ref[...] = grad * gate + dot(low, wi_ref[...], NT)


def gate_both(mixed, resid, grad, live, w_in, w_out):
    rows, wide = mixed.shape
    place = pl.BlockSpec(memory_space=pltpu.VMEM)
    return pl.pallas_call(
        gate_kernel,
        in_specs=[place, place, place, pl.BlockSpec(memory_space=pltpu.SMEM), place, place],
        out_specs=[place] * 4,
        out_shape=[
            jax.ShapeDtypeStruct((rows, wide), BF16),
            jax.ShapeDtypeStruct((rows, wide), F32),
            jax.ShapeDtypeStruct(w_in.shape, BF16),
            jax.ShapeDtypeStruct(w_out.shape, BF16),
        ],
        compiler_params=kernel_limits(60),
        cost_estimate=estimate(20 * rows * wide * w_in.shape[1], 30 * rows * wide),
        name="gate_both",
    )(mixed, resid, grad, live, w_in, w_out)


def bit_pairs(devices, bit):
    return [(index, index ^ (1 << bit)) for index in range(devices)]


def own_bit(bit):
    return (lax.axis_index("fsdp") >> bit) & 1


def gather_small(block, devices):
    gathered = block[None]
    for bit in range(devices.bit_length() - 1):
        other = lax.ppermute(gathered, "fsdp", bit_pairs(devices, bit))
        high = own_bit(bit) == 1
        gathered = jnp.where(
            high,
            jnp.concatenate((other, gathered), axis=0),
            jnp.concatenate((gathered, other), axis=0),
        )
    return gathered


def after(values, earlier):
    if not earlier:
        return list(values)
    return list(lax.optimization_barrier(tuple(values) + tuple(earlier))[: len(values)])


def swap(block, bits, devices):
    mask = sum(1 << bit for bit in bits)
    return lax.ppermute(block, "fsdp", [(index, index ^ mask) for index in range(devices)])


def axis_bits(devices):
    bits = devices.bit_length() - 1
    if bits == 5:
        return ((1,), (2,), (3, 4))
    span = (bits - 1 + 2) // 3
    places = tuple(range(1, bits))
    return (places[:span], places[span : 2 * span], places[2 * span :])


def subsets(bits):
    found = [()]
    for bit in bits:
        found = found + [each + (bit,) for each in found]
    return found


def mask_of(bits):
    return sum(1 << bit for bit in bits)


class Gatherer:
    def __init__(self, devices):
        self.devices = devices
        self.x_bits, self.y_bits, self.z_bits = axis_bits(devices)
        self.last = []
        self.ends = []

    def doubled(self, field, slots, bits):
        for bit in bits:
            other = swap(field, (bit,), self.devices)
            field = jnp.concatenate((field, other), axis=0)
            slots = slots + [slot ^ (1 << bit) for slot in slots]
        return (field, slots)

    def group(self, block, begin, end, middle):
        rows = block.shape[0]
        (own,) = after((block[None, :, begin:end],), self.last)
        fields, slots = ([own], [0])
        for bits in subsets(self.z_bits)[1:]:
            fields.append(swap(own, bits, self.devices))
            slots.append(mask_of(bits))
        plan, sources, firsts, seconds = ([], [], [], [])
        for first, last, left, right in (
            (self.x_bits, self.y_bits, begin, middle),
            (self.y_bits, self.x_bits, middle, end),
        ):
            field = jnp.concatenate(
                [each[:, :, left - begin : right - begin] for each in fields], axis=0
            )
            (field,) = after((field,), self.ends)
            firsts.append((*self.doubled(field, slots, first), last, left, right))
        self.last = [each[0] for each in firsts]
        self.ends = []
        for field, its_slots, last, left, right in firsts:
            held = [(field, its_slots)]
            for bit in last + (0,):
                if bit == 0:
                    self.ends += [part for part, _ in held[1:]]
                held = held + [
                    (swap(part, (bit,), self.devices), [slot ^ (1 << bit) for slot in part_slots])
                    for part, part_slots in held
                ]
            for part, part_slots in held:
                sources.append(part)
                plan.append((tuple(part_slots), rows, 0, left, right))
        return (plan, sources)

    def weight(self, block, groups):
        plan, sources = ([], [])
        rows = block.shape[0]
        if rows % 16:
            whole = lax.all_gather(block, "fsdp", axis=0, tiled=True)[None]
            plan = [((None,), rows * self.devices, begin, begin, end) for begin, _, end in groups]
            return (plan, [whole] * len(groups))
        for begin, middle, end in groups:
            more_plan, more_sources = self.group(block, begin, end, middle)
            plan += more_plan
            sources += more_sources
        return (plan, sources)


def take(field, axis, place):
    return lax.dynamic_index_in_dim(field, place, axis, keepdims=False)


def halved(field, held, bit, devices):
    axis = held.index(bit)
    mine = own_bit(bit)
    arrived = swap(take(field, axis, 1 - mine), (bit,), devices)
    return (take(field, axis, mine) + arrived, held[:axis] + held[axis + 1 :])


class Scatterer:
    def __init__(self, devices, *gradients):
        x_bits, y_bits, z_bits = axis_bits(devices)
        self.bits = devices.bit_length() - 1
        self.orders = (y_bits + x_bits + z_bits, x_bits + y_bits + z_bits)
        self.split = len(x_bits + y_bits)
        self.shapes = [mine.shape[1:] for mine, _ in gradients]
        self.width = math.gcd(*[shape[1] for shape in self.shapes])
        self.stage = -1
        self.kept = [mine for mine, _ in gradients]
        self.sends = [(theirs, 0) for _, theirs in gradients]
        self.result = None

    def prepare(self, parts, held):
        self.kept, self.sends = ([], [])
        self.held = []
        for place, part in enumerate(parts):
            bit = self.orders[place][self.stage]
            axis = held[place].index(bit)
            mine = own_bit(bit)
            self.kept.append(take(part, axis, mine))
            self.sends.append((take(part, axis, 1 - mine), bit))
            self.held.append(held[place][:axis] + held[place][axis + 1 :])

    def receive(self, arrived):
        totals = [
            kept.astype(F32) + other.astype(F32) for kept, other in zip(self.kept, arrived)
        ]
        self.stage += 1
        if self.stage == self.bits - 1:
            (total,) = totals
            self.sends, self.result = ([], [])
            begin = 0
            for rows, columns in self.shapes:
                pieces = []
                for _ in range(columns // self.width):
                    pieces.append(total[begin : begin + rows])
                    begin += rows
                self.result.append(jnp.concatenate(pieces, axis=1))
            return
        parts = [total.astype(BF16) for total in totals]
        if self.stage == 0:
            blocks = []
            for part in parts:
                for begin in range(0, part.shape[-1], self.width):
                    blocks.append(part[..., begin : begin + self.width])
            field = blocks[0] if len(blocks) == 1 else jnp.concatenate(blocks, axis=1)
            field = field.reshape((2,) * (self.bits - 1) + field.shape[1:])
            middle = self.width // 2
            parts = [field[..., :middle], field[..., middle:]]
            self.held = [list(range(self.bits - 1, 0, -1))] * 2
        if self.stage == self.split:
            parts = [jnp.concatenate(parts, axis=-1)]
        self.prepare(parts, self.held)


class Ticks:
    def __init__(self):
        self.before = []

    def run(self, groups, value, work):
        groups = [group for group in groups if group.result is None]
        sends = [each for group in groups for each in group.sends]
        value, *blocks = after([value] + [block for block, _ in sends], self.before)
        devices = lax.axis_size("fsdp")
        arrived = [swap(block, (bit,), devices) for block, (_, bit) in zip(blocks, sends)]
        outs = jax.tree.leaves(work(value))
        done = after(outs + arrived, [])
        if len(done) > 1:
            done = list(lax.optimization_barrier(tuple(done)))
        outs, arrived = (done[: len(outs)], done[len(outs) :])
        begin = 0
        for group in groups:
            count = len(group.sends)
            group.receive(arrived[begin : begin + count])
            begin += count
        self.before = outs[:1]
        return outs

    def finish(self, groups):
        while any(group.result is None for group in groups):
            self.run(groups, jnp.zeros((), F32), lambda value: value)


def halves(gradient, devices):
    pairs = gradient.reshape((devices // 2, 2) + gradient.shape[1:])
    mine = own_bit(0)
    return (take(pairs, 1, mine), take(pairs, 1, 1 - mine))


def shards(
    x_vit,
    x_hires,
    image_live,
    grad_vit,
    grad_hires,
    gain_one,
    w_qkv,
    w_out,
    gain_two,
    w_up,
    w_down,
    conv_seven,
    gain_three,
    w_expand,
    w_shrink,
    layer_scale,
    w_adapt,
    conv_three,
    w_gate_in,
    w_gate_out,
):
    devices = lax.axis_size("fsdp")
    edge_c, edge_d = (gain_three.shape[0], gain_one.shape[0])
    small = jnp.concatenate(
        (
            conv_seven.reshape(-1),
            gain_three,
            layer_scale,
            conv_three.reshape(-1),
            gain_one,
            gain_two,
        )
    )
    small_all = gather_small(small, devices)
    marks = [0]
    for length in (KS * KS * edge_c, edge_c, edge_c, KA * KA * edge_d, edge_d, edge_d):
        marks.append(marks[-1] + length)
    small_parts = [small_all[:, marks[place] : marks[place + 1]] for place in range(6)]
    seven_taps = small_parts[0].reshape(devices, KS * KS, edge_c).swapaxes(0, 1).reshape(KS * KS, C)
    three_taps = small_parts[3].reshape(devices, KA * KA, edge_d).swapaxes(0, 1).reshape(KA * KA, D)
    gain_c, scale_c = (small_parts[1].reshape(C).astype(F32), small_parts[2].reshape(C).astype(F32))
    gain_a, gain_b = (small_parts[4].reshape(D).astype(F32), small_parts[5].reshape(D).astype(F32))

    me = lax.axis_index("fsdp").astype(jnp.int32).reshape(1)
    def gathered(block):
        return lax.all_gather(block, "fsdp", axis=0, tiled=True)

    vit_all = gathered(jnp.concatenate((w_qkv, w_out, w_gate_in, w_gate_out), axis=1))
    qkv_all = vit_all[:, : 3 * D]
    out_all = vit_all[:, 3 * D : 4 * D]
    gate_in_all = vit_all[:, 4 * D : 5 * D]
    gate_out_all = vit_all[:, 5 * D :]
    up_all = gathered(w_up)
    down_all = gathered(w_down)
    adapt_all = gathered(w_adapt)
    live = image_live.astype(F32)
    grad_joined_low = (grad_vit.astype(F32) * live).astype(BF16)
    patch_in = x_vit.astype(F32)

    gatherer = Gatherer(devices)
    expand_pieces = gatherer.weight(w_expand, [(0, D, 2 * D), (2 * D, 3 * D, 4 * D)])
    conved = depthwise(after((x_hires,), gatherer.last)[0], seven_taps, KS, GRID_HR)
    gatherer.ends.append(conved)
    more_pieces = gatherer.weight(w_expand, [(4 * D, 5 * D, 6 * D)])
    normed_a, inverse_a = norm_rows(patch_in, 1e-05)
    normed_a_low = (normed_a * gain_a).astype(BF16)
    normed_a_low = after((normed_a_low,), gatherer.last)[0]
    qkv_low = dot(normed_a_low, qkv_all, NN).astype(BF16)
    attended_low = attend(qkv_low)
    gatherer.ends.append(attended_low)
    shrink_pieces = gatherer.weight(w_shrink, [(0, C // 4, C // 2), (C // 2, 3 * C // 4, C)])
    expand_pieces = tuple(one + two for one, two in zip(expand_pieces, more_pieces))

    def shares(gradient):
        return gradient.reshape(devices, gradient.shape[0] // devices, gradient.shape[1])

    def split(gradient):
        if len(gradient) == 2:
            return tuple(gradient)
        return halves(shares(gradient[0]), devices)

    resid_one = patch_in + dot(attended_low, out_all, NN)
    normed_b, inverse_b = norm_rows(resid_one, 1e-05)
    normed_b_low = (normed_b * gain_b).astype(BF16)
    normed_b_low = after((normed_b_low,), expand_pieces[1] + shrink_pieces[1])[0]
    mlp_out, grad_b, d_up, d_down = mlp_both(
        grad_joined_low, normed_b_low, up_all, down_all, me, devices, D
    )
    resid_two = resid_one + mlp_out
    d_gain_two = jnp.sum(grad_b * normed_b, axis=0)
    grad_first = grad_joined_low.astype(F32) + norm_back(grad_b * gain_b, normed_b, inverse_b)
    ticks = Ticks()
    sum_mlp = Scatterer(devices, split(d_up), split(d_down))

    def attention_back(grad_first):
        grad_first_low = grad_first.astype(BF16)
        d_out = dot(attended_low, grad_first_low, TN).astype(BF16)
        grad_att_low = dot(grad_first_low, out_all, NT).astype(BF16)
        grad_qkv_low = jnp.concatenate(attend_back(qkv_low, grad_att_low), axis=1)
        d_qkv = dot(normed_a_low, grad_qkv_low, TN).astype(BF16)
        grad_a = dot(grad_qkv_low, qkv_all, NT)
        d_gain_one = jnp.sum(grad_a * normed_a, axis=0)
        grad_patches = grad_first + norm_back(grad_a * gain_a, normed_a, inverse_a)
        return (grad_patches, d_gain_one, d_qkv, d_out)

    grad_patches, d_gain_one, d_qkv, d_out = ticks.run([sum_mlp], grad_first, attention_back)
    sum_attention = Scatterer(devices, split((d_qkv,)), split((d_out,)))

    normed_c, inverse_c = norm_rows(conved, 1e-06)
    normed_c_low = (normed_c * gain_c).astype(BF16)
    tile = D
    tiles = w_expand.shape[1] // tile

    def network(field):
        return mlp_forward(
            field, expand_pieces, shrink_pieces, me, w_expand.shape[1], w_expand.shape[1], tile, 256
        )

    shrunk, activated, slope, expand_all, shrink_all = (
        lambda outs: (outs[2], outs[0], outs[1], outs[3], outs[4])
    )(ticks.run([sum_mlp, sum_attention], normed_c_low, network))

    table = pool_table(GRID_HR, GRID_LR)
    pool = jnp.einsum("ia,jb->ijab", table, table).reshape(GRID_LR**2, GRID_HR**2).astype(BF16)

    def adapter(shrunk):
        hires_out = x_hires.astype(F32) + scale_c * shrunk
        pooled_low = dot(pool, hires_out.astype(BF16), NN).astype(BF16)
        adapted = dot(pooled_low, adapt_all, NN)
        mixed = depthwise(adapted, three_taps, KA, GRID_LR)
        joined, grad_mixed, d_gate_in, d_gate_out = gate_both(
            mixed, resid_two, grad_vit, image_live, gate_in_all, gate_out_all
        )
        hires_next = (live * hires_out).astype(BF16)
        return (grad_mixed, d_gate_in, d_gate_out, joined, hires_next, pooled_low, adapted)

    grad_mixed, d_gate_in, d_gate_out, joined, hires_next, pooled_low, adapted = ticks.run(
        [sum_mlp, sum_attention], shrunk, adapter
    )

    def adapter_back(grad_mixed):
        grad_adapted_low, d_conv_three = depthwise_back(
            grad_mixed, adapted, jnp.zeros(adapted.shape, BF16), three_taps, KA, GRID_LR, 0, D
        )
        d_adapt = dot(pooled_low, grad_adapted_low, TN).astype(BF16)
        grad_pooled_low = dot(grad_adapted_low, adapt_all, NT).astype(BF16)
        grad_hires_out = live * grad_hires.astype(F32) + dot(pool, grad_pooled_low, TN)
        d_layer_scale = jnp.sum(grad_hires_out * shrunk, axis=0)
        grad_shrunk_low = (grad_hires_out * scale_c).astype(BF16)
        return (grad_shrunk_low, d_layer_scale, grad_hires_out, d_adapt, d_conv_three)

    grad_shrunk_low, d_layer_scale, grad_hires_out, d_adapt, d_conv_three = ticks.run(
        [sum_mlp, sum_attention], grad_mixed, adapter_back
    )
    square = jnp.concatenate((shares(d_gate_in), shares(d_gate_out), shares(d_adapt)), axis=1)
    sum_square = Scatterer(devices, halves(square, devices))

    outs = ticks.run(
        [sum_mlp, sum_attention, sum_square],
        grad_shrunk_low,
        lambda grad: outer_sum(activated, grad, me, w_shrink.shape[0]),
    )
    sum_shrink = Scatterer(devices, tuple(outs))
    grad_c = jnp.zeros((x_hires.shape[0], C), F32)
    beside = ([sum_attention, sum_square, sum_shrink], [sum_shrink], [sum_shrink, sum_square])
    sums_expand = []
    for part in range(3):
        grad_c, *d_part = ticks.run(
            list(beside[part]) + sums_expand[-1:],
            grad_c,
            lambda start, part=part: mlp_back(
                grad_shrunk_low,
                normed_c_low,
                slope,
                expand_all,
                shrink_all,
                start,
                me,
                devices,
                tile,
                256,
                part * tiles // 3,
                (part + 1) * tiles // 3,
            ),
        )
        sums_expand.append(Scatterer(devices, split(d_part)))
    d_gain_three = jnp.sum(grad_c * normed_c, axis=0)
    grad_conved = norm_back(grad_c * gain_c, normed_c, inverse_c)
    grad_hires_in = grad_hires_out
    pieces_seven = []
    width = C // 3
    beside = (
        [sum_shrink, sum_square, sums_expand[0], sums_expand[2]],
        [sum_shrink, sums_expand[0], sums_expand[1]],
        [sum_square, sums_expand[1], sums_expand[2]],
    )
    for part in range(3):
        grad_hires_in, taps_part = ticks.run(
            beside[part],
            grad_hires_in,
            lambda base, part=part: depthwise_back(
                grad_conved,
                x_hires,
                base,
                seven_taps,
                KS,
                GRID_HR,
                part * width,
                (part + 1) * width,
            ),
        )
        pieces_seven.append(taps_part)
    d_conv_seven = jnp.concatenate(pieces_seven, axis=1)
    ticks.finish([sum_mlp, sum_attention, sum_square, sum_shrink] + sums_expand)
    g_up, g_down = sum_mlp.result
    g_qkv, g_out = sum_attention.result
    (g_square,) = sum_square.result
    (g_shrink,) = sum_shrink.result
    g_expand = jnp.concatenate([each.result[0] for each in sums_expand], axis=1)

    small_grads = jnp.concatenate(
        (
            d_conv_seven.reshape(KS * KS, devices, edge_c).swapaxes(0, 1).reshape(devices, -1),
            d_gain_three.reshape(devices, edge_c),
            d_layer_scale.reshape(devices, edge_c),
            d_conv_three.reshape(KA * KA, devices, edge_d).swapaxes(0, 1).reshape(devices, -1),
            d_gain_one.reshape(devices, edge_d),
            d_gain_two.reshape(devices, edge_d),
        ),
        axis=1,
    )
    small_sums = small_grads.reshape((2,) * (devices.bit_length() - 1) + small_grads.shape[1:])
    held = list(range(devices.bit_length() - 2, -1, -1))
    for bit in range(devices.bit_length() - 1):
        small_sums, held = halved(small_sums, held, bit, devices)
    small_outs = [small_sums[marks[place] : marks[place + 1]] for place in range(6)]
    return (
        joined,
        hires_next,
        grad_patches,
        grad_hires_in,
        small_outs[4],
        g_qkv,
        g_out,
        small_outs[5],
        g_up,
        g_down,
        small_outs[0].reshape(KS * KS, edge_c),
        small_outs[1],
        g_expand,
        g_shrink,
        small_outs[2],
        g_square[2 * edge_d :],
        small_outs[3].reshape(KA * KA, edge_d),
        g_square[:edge_d],
        g_square[edge_d : 2 * edge_d],
    )


def solution(mesh):
    in_specs = (
        P("fsdp", None),
        P("fsdp", None),
        P("fsdp"),
        P("fsdp", None),
        P("fsdp", None),
        P("fsdp"),
        P("fsdp", None),
        P("fsdp", None),
        P("fsdp"),
        P("fsdp", None),
        P("fsdp", None),
        P(None, "fsdp"),
        P("fsdp"),
        P("fsdp", None),
        P("fsdp", None),
        P("fsdp"),
        P("fsdp", None),
        P(None, "fsdp"),
        P("fsdp", None),
        P("fsdp", None),
    )
    out_specs = (
        P("fsdp", None),
        P("fsdp", None),
        P("fsdp", None),
        P("fsdp", None),
        P("fsdp"),
        P("fsdp", None),
        P("fsdp", None),
        P("fsdp"),
        P("fsdp", None),
        P("fsdp", None),
        P(None, "fsdp"),
        P("fsdp"),
        P("fsdp", None),
        P("fsdp", None),
        P("fsdp"),
        P("fsdp", None),
        P(None, "fsdp"),
        P("fsdp", None),
        P("fsdp", None),
    )
    return jax.shard_map(shards, mesh=mesh, in_specs=in_specs, out_specs=out_specs, check_vma=False)
```

```python
import functools
import math

import jax
import jax.numpy as jnp
from jax import lax
from jax.experimental import pallas as pl
from jax.experimental.pallas import tpu as pltpu
from jax.sharding import PartitionSpec as P

D = 1024
HEAD_DIM = 64
C = 1536
KS = 7
KA = 3
GRID_LR = 24
GRID_HR = 32
LANES = 128
GROUP = 8
NN = ((1,), (0,))
NT = ((1,), (1,))
TN = ((0,), (0,))
BF16 = jnp.bfloat16
F32 = jnp.float32


def dot(left, right, dims):
    return lax.dot_general(left, right, (dims, ((), ())), preferred_element_type=F32)


def kernel_limits(mebibytes):
    return pltpu.CompilerParams(vmem_limit_bytes=mebibytes * 2**20)


def estimate(flops, moved):
    return pl.CostEstimate(flops=flops, bytes_accessed=moved, transcendentals=0)


def norm_rows(values, epsilon):
    average = jnp.mean(values, axis=-1, keepdims=True)
    centred = values - average
    spread = jnp.mean(centred * centred, axis=-1, keepdims=True)
    inverse = lax.rsqrt(spread + epsilon)
    return (centred * inverse, inverse)


def norm_back(grad_normed, normed, inverse):
    first_mean = jnp.mean(grad_normed, axis=-1, keepdims=True)
    second_mean = jnp.mean(grad_normed * normed, axis=-1, keepdims=True)
    return inverse * (grad_normed - first_mean - normed * second_mean)


def gelu_pair(values):
    cdf = 0.5 * (1.0 + lax.erf(values * (1.0 / math.sqrt(2.0))))
    density = jnp.exp(-0.5 * values * values) * (1.0 / math.sqrt(2.0 * math.pi))
    return (values * cdf, cdf + values * density)


def pool_table(fine_cells, coarse_cells):
    coarse_index = jnp.arange(coarse_cells, dtype=jnp.int32)[:, None]
    fine_index = jnp.arange(fine_cells, dtype=jnp.int32)[None, :]
    window_start = coarse_index * fine_cells // coarse_cells
    window_end = ((coarse_index + 1) * fine_cells + coarse_cells - 1) // coarse_cells
    inside = ((fine_index >= window_start) & (fine_index < window_end)).astype(jnp.float32)
    return inside / jnp.sum(inside, axis=1, keepdims=True)


def fill_shifted(shifted, field, width, edge):
    reach = width // 2
    cells, lanes = field.shape
    column = lax.broadcasted_iota(jnp.int32, (cells, lanes), 0) % edge
    for step in range(width):
        offset = step - reach
        moved = field
        if offset != 0:
            moved = pltpu.roll(field, (-offset) % cells, 0)
            inside = (column + offset >= 0) & (column + offset < edge)
            moved = jnp.where(inside, moved, 0.0)
        shifted[step, reach : reach + edge] = moved.reshape(edge, edge, lanes)


def clear_edges(shifted, width, edge):
    reach = width // 2
    border = jnp.zeros((width, reach) + shifted.shape[2:], F32)
    shifted[:, 0:reach] = border
    shifted[:, reach + edge :] = border


def depthwise_kernel(width, edge, field_ref, taps_ref, out_ref, shifted, wide):
    @pl.when(pl.program_id(0) == 0)
    def _():
        clear_edges(shifted, width, edge)

    fill_shifted(shifted, field_ref[...].astype(F32), width, edge)
    wide[...] = jnp.broadcast_to(taps_ref[...].astype(F32)[:, None, :], wide.shape)
    strips = edge // 8

    def body(index, carry):
        base = (index // strips) * GROUP
        column = pl.multiple_of((index % strips) * 8, 8)
        sums = [jnp.zeros((8, LANES), F32)] * GROUP
        for step in range(width):
            taps = [wide[tap * width + step] for tap in range(width)]
            for row in range(GROUP + width - 1):
                value = shifted[step, base + row, pl.ds(column, 8), :]
                for place in range(GROUP):
                    if 0 <= row - place < width:
                        sums[place] = sums[place] + value * taps[row - place]
        for place in range(GROUP):
            start = pl.multiple_of((base + place) * edge + column, 8)
            out_ref[pl.ds(start, 8), :] = sums[place]
        return carry

    lax.fori_loop(0, (edge // GROUP) * strips, body, 0)


def depthwise(field, taps, width, edge):
    cells, channels = field.shape
    return pl.pallas_call(
        functools.partial(depthwise_kernel, width, edge),
        grid=(channels // LANES,),
        in_specs=[
            pl.BlockSpec((cells, LANES), lambda i: (0, i)),
            pl.BlockSpec((width * width, LANES), lambda i: (0, i)),
        ],
        out_specs=pl.BlockSpec((cells, LANES), lambda i: (0, i)),
        out_shape=jax.ShapeDtypeStruct((cells, channels), F32),
        scratch_shapes=[
            pltpu.VMEM((width, edge + width - 1, edge, LANES), F32),
            pltpu.VMEM((width * width, 8, LANES), F32),
        ],
        compiler_params=kernel_limits(32),
        cost_estimate=estimate(600 * width * width * cells * channels, 8 * cells * channels),
        name="depthwise",
    )(field, taps)


def depthwise_back_kernel(
    width, edge, grad_ref, field_ref, base_ref, taps_ref, out_ref, tap_out_ref, shifted, wide, cells_ref, sums_ref
):
    @pl.when(pl.program_id(0) == 0)
    def _():
        clear_edges(shifted, width, edge)

    fill_shifted(shifted, grad_ref[...], width, edge)
    cells_ref[...] = field_ref[...].astype(F32)
    sums_ref[...] = base_ref[...].astype(F32)
    wide[...] = jnp.broadcast_to(taps_ref[...].astype(F32)[:, None, :], wide.shape)
    strips = edge // 8
    last = width - 1

    for step in range(width):
        taps = [wide[(last - tap) * width + (last - step)] for tap in range(width)]

        def body(index, tap_sums):
            tap_sums = list(tap_sums)
            base = (index // strips) * GROUP
            column = pl.multiple_of((index % strips) * 8, 8)
            spots = [
                pl.ds(pl.multiple_of((base + place) * edge + column, 8), 8)
                for place in range(GROUP)
            ]
            sums = [sums_ref[spot, :] for spot in spots]
            cells = [cells_ref[spot, :] for spot in spots]
            for row in range(GROUP + width - 1):
                value = shifted[step, base + row, pl.ds(column, 8), :]
                for place in range(GROUP):
                    tap = row - place
                    if 0 <= tap < width:
                        sums[place] = sums[place] + value * taps[tap]
                        tap_sums[tap] = tap_sums[tap] + value * cells[place]
            for place in range(GROUP):
                sums_ref[spots[place], :] = sums[place]
            return tuple(tap_sums)

        tap_sums = lax.fori_loop(
            0, (edge // GROUP) * strips, body, (jnp.zeros((8, LANES), F32),) * width
        )
        for tap in range(width):
            spot = (last - tap) * width + (last - step)
            tap_out_ref[spot : spot + 1, :] = jnp.sum(tap_sums[tap], axis=0, keepdims=True)
    out_ref[...] = sums_ref[...].astype(out_ref.dtype)


def depthwise_back(grad, field, base, taps, width, edge, first, last):
    cells, channels = field.shape
    skip = first // LANES
    full = pl.BlockSpec((cells, LANES), lambda i: (0, i + skip))
    small = pl.BlockSpec((width * width, LANES), lambda i: (0, i + skip))
    return pl.pallas_call(
        functools.partial(depthwise_back_kernel, width, edge),
        grid=((last - first) // LANES,),
        in_specs=[full, full, full, small],
        out_specs=[full, pl.BlockSpec((width * width, LANES), lambda i: (0, i))],
        out_shape=[
            jax.ShapeDtypeStruct((cells, channels), base.dtype),
            jax.ShapeDtypeStruct((width * width, last - first), F32),
        ],
        scratch_shapes=[
            pltpu.VMEM((width, edge + width - 1, edge, LANES), F32),
            pltpu.VMEM((width * width, 8, LANES), F32),
            pltpu.VMEM((cells, LANES), F32),
            pltpu.VMEM((cells, LANES), F32),
        ],
        input_output_aliases={2: 0},
        compiler_params=kernel_limits(32),
        cost_estimate=estimate(
            1200 * width * width * cells * (last - first), 14 * cells * (last - first)
        ),
        name="depthwise_back",
    )(grad, field, base, taps)


def softmax_rows(query, key):
    scores = dot(query, key, NT) * HEAD_DIM ** (-0.5)
    raised = jnp.exp(scores - jnp.max(scores, axis=-1, keepdims=True))
    return raised * (1.0 / jnp.sum(raised, axis=-1, keepdims=True))


def attend_kernel(q_ref, k_ref, v_ref, out_ref):
    outs = []
    for head in range(out_ref.shape[1] // HEAD_DIM):
        lanes = slice(head * HEAD_DIM, (head + 1) * HEAD_DIM)
        probs = softmax_rows(q_ref[:, lanes], k_ref[:, lanes]).astype(BF16)
        outs.append(dot(probs, v_ref[:, lanes], NN))
    out_ref[...] = jnp.concatenate(outs, axis=1).astype(BF16)


def attend(qkv, width=256):
    rows = qkv.shape[0]
    steps = D // width

    def spec(part):
        return pl.BlockSpec((rows, width), lambda i: (0, i + part * steps))

    return pl.pallas_call(
        attend_kernel,
        grid=(steps,),
        in_specs=[spec(0), spec(1), spec(2)],
        out_specs=spec(0),
        out_shape=jax.ShapeDtypeStruct((rows, D), BF16),
        compiler_params=kernel_limits(48),
        cost_estimate=estimate(40 * rows * rows * D, 8 * rows * D),
        name="attend",
    )(qkv, qkv, qkv)


def attend_back_kernel(q_ref, k_ref, v_ref, g_ref, dq_ref, dk_ref, dv_ref):
    scale = HEAD_DIM ** (-0.5)
    dqs, dks, dvs = ([], [], [])
    for head in range(dq_ref.shape[1] // HEAD_DIM):
        lanes = slice(head * HEAD_DIM, (head + 1) * HEAD_DIM)
        query, key, value, grad = (q_ref[:, lanes], k_ref[:, lanes], v_ref[:, lanes], g_ref[:, lanes])
        probs = softmax_rows(query, key)
        grad_probs = dot(grad, value, NT)
        dvs.append(dot(probs.astype(BF16), grad, TN))
        total = jnp.sum(probs * grad_probs, axis=-1, keepdims=True)
        low = (probs * (grad_probs - total)).astype(BF16)
        dqs.append(dot(low, key, NN) * scale)
        dks.append(dot(low, query, TN) * scale)
    dq_ref[...] = jnp.concatenate(dqs, axis=1).astype(BF16)
    dk_ref[...] = jnp.concatenate(dks, axis=1).astype(BF16)
    dv_ref[...] = jnp.concatenate(dvs, axis=1).astype(BF16)


def attend_back(qkv, grad, width=256):
    rows = qkv.shape[0]
    steps = D // width

    def spec(part):
        return pl.BlockSpec((rows, width), lambda i: (0, i + part * steps))

    return pl.pallas_call(
        attend_back_kernel,
        grid=(steps,),
        in_specs=[spec(0), spec(1), spec(2), spec(0)],
        out_specs=[spec(0)] * 3,
        out_shape=[jax.ShapeDtypeStruct((rows, D), BF16)] * 3,
        compiler_params=kernel_limits(48),
        cost_estimate=estimate(70 * rows * rows * D, 14 * rows * D),
        name="attend_back",
    )(qkv, qkv, qkv, grad)


def start_copies(plan, me, sources, target, semaphore, first=0, last=None):
    for source, (slots, rows, offset, begin, end) in zip(sources, plan):
        left, right = (max(begin, first), end if last is None else min(end, last))
        if left >= right:
            continue
        for place, slot in enumerate(slots):
            line = 0 if slot is None else pl.multiple_of((me ^ slot) * rows, rows)
            pltpu.make_async_copy(
                source.at[place, :, pl.ds(left - begin + offset, right - left)],
                target.at[pl.ds(line, rows), pl.ds(left - first, right - left)],
                semaphore,
            ).start()


def store_shares(value, rows, even, mine_ref, theirs_ref, lines=slice(None)):
    low = value.astype(BF16).reshape(-1, 2, rows, value.shape[-1])

    @pl.when(even)
    def _():
        mine_ref[lines] = low[:, 0]
        theirs_ref[lines] = low[:, 1]

    @pl.when(jnp.logical_not(even))
    def _():
        mine_ref[lines] = low[:, 1]
        theirs_ref[lines] = low[:, 0]


def share_type(devices, rows, columns):
    return jax.ShapeDtypeStruct((devices // 2, rows, columns), BF16)


SCALARS = pl.BlockSpec(memory_space=pltpu.SMEM)
ANYWHERE = pl.BlockSpec(memory_space=pl.ANY)
LOCAL = pl.BlockSpec(memory_space=pltpu.VMEM)


def mlp_both_kernel(shares, me_ref, g_ref, h_ref, wi_ref, wo_ref, out_ref, dh_ref, *grads):
    @pl.when(pl.program_id(0) == 0)
    def _():
        out_ref[...] = jnp.zeros_like(out_ref)
        dh_ref[...] = jnp.zeros_like(dh_ref)

    hidden = dot(h_ref[...], wi_ref[...], NN)
    back = dot(g_ref[...], wo_ref[...], NT)
    act, slope = gelu_pair(hidden)
    act = act.astype(BF16)
    out_ref[...] += dot(act, wo_ref[...], NN)
    low = (back * slope).astype(BF16)
    dh_ref[...] += dot(low, wi_ref[...], NT)
    even = me_ref[0] % 2 == 0
    if shares[0]:
        store_shares(dot(h_ref[...], low, TN), shares[0], even, *grads[:2])
    else:
        grads[0][...] = dot(h_ref[...], low, TN).astype(BF16)
    store_shares(dot(act, g_ref[...], TN), shares[1], even, *grads[-2:])


def mlp_both(grad, field, w_in, w_out, me, devices, tile):
    rows, wide = field.shape
    hidden = w_out.shape[0]
    whole = pl.BlockSpec((rows, wide), lambda i: (0, 0), pipeline_mode=pl.Buffered(1))
    total = pl.BlockSpec((rows, wide), lambda i: (0, 0))
    columns = pl.BlockSpec((wide, tile), lambda i: (0, i))
    in_rows, out_rows = (wide // devices, hidden // devices)
    in_specs = [pl.BlockSpec((devices // 2, in_rows, tile), lambda i: (0, 0, i))] * 2
    in_types = [share_type(devices, in_rows, hidden)] * 2
    if in_rows % 16:
        in_rows = 0
        in_specs = [columns]
        in_types = [jax.ShapeDtypeStruct((wide, hidden), BF16)]
    out_block = pl.BlockSpec((tile // out_rows // 2, out_rows, wide), lambda i: (i, 0, 0))
    outs = pl.pallas_call(
        functools.partial(mlp_both_kernel, (in_rows, out_rows)),
        grid=(hidden // tile,),
        in_specs=[SCALARS, whole, whole, columns, pl.BlockSpec((tile, wide), lambda i: (i, 0))],
        out_specs=[total, total] + in_specs + [out_block] * 2,
        out_shape=[
            jax.ShapeDtypeStruct((rows, wide), F32),
            jax.ShapeDtypeStruct((rows, wide), F32),
        ]
        + in_types
        + [share_type(devices, out_rows, wide)] * 2,
        compiler_params=kernel_limits(60),
        cost_estimate=estimate(14 * rows * wide * hidden, 8 * wide * hidden),
        name="mlp_both",
    )(me, grad, field, w_in, w_out)
    return (outs[0], outs[1], outs[2:-2], outs[-2:])


def expand_kernel(plan, tile, tiles, rows, me_ref, h_ref, *refs):
    sources = refs[: len(plan)]
    act_ref, slope_ref, natural, weights, sems = refs[len(plan) :]
    step = pl.program_id(0)
    me = me_ref[0]

    def load(number):
        slot = number % 2
        start_copies(
            plan, me, sources, weights.at[slot], sems.at[slot], number * tile, (number + 1) * tile
        )

    def save(number, slot):
        return pltpu.make_async_copy(
            weights.at[slot],
            natural.at[:, pl.ds(pl.multiple_of(number * tile, tile), tile)],
            sems.at[2 + slot],
        )

    @pl.when(step == 0)
    def _():
        load(0)

    slot = step % 2
    pltpu.make_async_copy(weights.at[slot], weights.at[slot], sems.at[slot]).wait()
    save(step, slot).start()

    @pl.when(step > 0)
    def _():
        save(step - 1, 1 - slot).wait()

    for number in range(1, tiles):

        @pl.when(step == number - 1)
        def _():
            load(number)

    def body(index, carry):
        spot = pl.ds(pl.multiple_of(index * rows, rows), rows)
        act, slope = gelu_pair(dot(h_ref[spot, :], weights[slot], NN))
        act_ref[spot, :] = act.astype(BF16)
        slope_ref[spot, :] = slope.astype(BF16)
        return carry

    lax.fori_loop(0, h_ref.shape[0] // rows, body, 0)

    @pl.when(step == tiles - 1)
    def _():
        save(step, slot).wait()


def expand(field, pieces, me, hidden, tile, step):
    plan, sources = pieces
    rows, wide = field.shape
    whole = pl.BlockSpec((rows, wide), lambda i: (0, 0), pipeline_mode=pl.Buffered(1))
    tiles = pl.BlockSpec((rows, tile), lambda i: (0, i))
    return pl.pallas_call(
        functools.partial(expand_kernel, plan, tile, hidden // tile, step),
        grid=(hidden // tile,),
        in_specs=[SCALARS, whole] + [ANYWHERE] * len(sources),
        out_specs=[tiles, tiles, ANYWHERE],
        out_shape=[
            jax.ShapeDtypeStruct((rows, hidden), BF16),
            jax.ShapeDtypeStruct((rows, hidden), BF16),
            jax.ShapeDtypeStruct((wide, hidden), BF16),
        ],
        scratch_shapes=[pltpu.VMEM((2, wide, tile), BF16), pltpu.SemaphoreType.DMA((4,))],
        compiler_params=kernel_limits(60),
        cost_estimate=estimate(4 * rows * wide * hidden, 4 * wide * hidden + 4 * rows * hidden),
        name="expand",
    )(me, field, *sources)


def shrink_kernel(plan, width, me_ref, live_ref, a_ref, x_ref, scale_ref, *refs):
    sources = refs[: len(plan)]
    out_ref, low_ref, next_ref, natural, weights, sems = refs[len(plan) :]
    live = live_ref[0].astype(F32)
    step = pl.program_id(0)
    parts = weights.shape[0]

    @pl.when(step == 0)
    def _():
        for place in range(parts):
            start_copies(
                plan,
                me_ref[0],
                sources,
                weights.at[place],
                sems.at[place],
                place * width,
                (place + 1) * width,
            )

    pltpu.make_async_copy(weights.at[step], weights.at[step], sems.at[step]).wait()
    save = pltpu.make_async_copy(
        weights.at[step],
        natural.at[:, pl.ds(pl.multiple_of(step * width, width), width)],
        sems.at[parts],
    )
    save.start()
    rows = 256

    def body(index, carry):
        spot = pl.ds(pl.multiple_of(index * rows, rows), rows)
        value = dot(a_ref[spot, :], weights[step], NN)
        out_ref[spot, :] = value
        hires = x_ref[spot, :].astype(F32) + scale_ref[...] * value
        low_ref[spot, :] = hires.astype(BF16)
        next_ref[spot, :] = (live * hires).astype(BF16)
        return carry

    lax.fori_loop(0, a_ref.shape[0] // rows, body, 0)
    save.wait()


def shrink(act, field, scale, live, pieces, me, width):
    plan, sources = pieces
    rows, hidden = act.shape
    columns = max(each[4] for each in plan)
    return pl.pallas_call(
        functools.partial(shrink_kernel, plan, width),
        grid=(columns // width,),
        in_specs=[
            SCALARS,
            SCALARS,
            pl.BlockSpec((rows, hidden), lambda i: (0, 0), pipeline_mode=pl.Buffered(1)),
            pl.BlockSpec((rows, width), lambda i: (0, i)),
            pl.BlockSpec((1, width), lambda i: (0, i)),
        ]
        + [ANYWHERE] * len(sources),
        out_specs=[pl.BlockSpec((rows, width), lambda i: (0, i))] * 3 + [ANYWHERE],
        out_shape=[
            jax.ShapeDtypeStruct((rows, columns), F32),
            jax.ShapeDtypeStruct((rows, columns), BF16),
            jax.ShapeDtypeStruct((rows, columns), BF16),
            jax.ShapeDtypeStruct((hidden, columns), BF16),
        ],
        scratch_shapes=[
            pltpu.VMEM((columns // width, hidden, width), BF16),
            pltpu.SemaphoreType.DMA((columns // width + 1,)),
        ],
        compiler_params=kernel_limits(60),
        cost_estimate=estimate(3 * rows * hidden * columns, 6 * hidden * columns),
        name="shrink",
    )(me, live, act, field, scale, *sources)


def outer_kernel(shares, me_ref, left_ref, right_ref, mine_ref, theirs_ref):
    value = dot(left_ref[...], right_ref[...], TN)
    store_shares(value, shares, me_ref[0] % 2 == 0, mine_ref, theirs_ref)


def outer_sum(left, right, me, share):
    rows, lines = left.shape
    columns = right.shape[1]
    if share % 16:
        return halves(dot(left, right, TN).astype(BF16).reshape(-1, share, columns), lines // share)
    tile = 4 * share if share >= 192 else 16 * share
    while lines % tile:
        tile //= 2
    block = pl.BlockSpec((tile // share // 2, share, columns), lambda i: (i, 0, 0))
    return pl.pallas_call(
        functools.partial(outer_kernel, share),
        grid=(lines // tile,),
        in_specs=[
            SCALARS,
            pl.BlockSpec((rows, tile), lambda i: (0, i)),
            pl.BlockSpec((rows, columns), lambda i: (0, 0), pipeline_mode=pl.Buffered(1)),
        ],
        out_specs=[block] * 2,
        out_shape=[share_type(lines // share, share, columns)] * 2,
        compiler_params=kernel_limits(48),
        cost_estimate=estimate(3 * rows * lines * columns, 2 * lines * columns),
        name="outer_sum",
    )(me, left, right)


def mlp_back_kernel(step, share, begun, me_ref, g_ref, h_ref, slope_ref, wi_ref, wo_ref, *refs):
    start_ref, dh_ref, *grads, low_ref = refs if begun else (None,) + refs

    @pl.when(pl.program_id(0) == 0)
    def _():
        dh_ref[...] = start_ref[...] if begun else jnp.zeros_like(dh_ref)

    def body(index, carry):
        spot = pl.ds(pl.multiple_of(index * step, step), step)
        back = dot(g_ref[spot, :], wo_ref[...], NT)
        low = (back * slope_ref[spot, :].astype(F32)).astype(BF16)
        low_ref[spot, :] = low
        dh_ref[spot, :] += dot(low, wi_ref[...], NT)
        return carry

    lax.fori_loop(0, h_ref.shape[0] // step, body, 0)
    block = h_ref.shape[1]
    even = me_ref[0] % 2 == 0

    def outer(index, carry):
        spot = pl.ds(pl.multiple_of(index * block, block), block)
        value = dot(h_ref[:, spot], low_ref[...], TN)
        if share:
            pairs = block // share // 2
            store_shares(value, share, even, *grads, pl.ds(index * pairs, pairs))
        else:
            grads[0][spot, :] = value.astype(BF16)
        return carry

    lax.fori_loop(0, h_ref.shape[1] // block, outer, 0)


def mlp_back(grad, field, slope, w_in, w_out, start, me, devices, tile, step, first, last):
    rows, wide = field.shape
    width = (last - first) * tile
    whole = pl.BlockSpec((rows, wide), lambda i: (0, 0), pipeline_mode=pl.Buffered(1))
    share = wide // devices
    grad_specs = [pl.BlockSpec((devices // 2, share, tile), lambda i: (0, 0, i))] * 2
    grad_types = [share_type(devices, share, width)] * 2
    if share % 16:
        share = 0
        grad_specs = [pl.BlockSpec((wide, tile), lambda i: (0, i))]
        grad_types = [jax.ShapeDtypeStruct((wide, width), BF16)]
    outs = pl.pallas_call(
        functools.partial(mlp_back_kernel, step, share, start is not None),
        grid=(last - first,),
        in_specs=[
            SCALARS,
            whole,
            whole,
            pl.BlockSpec((rows, tile), lambda i: (0, i + first)),
            pl.BlockSpec((wide, tile), lambda i: (0, i + first)),
            pl.BlockSpec((tile, wide), lambda i: (i + first, 0)),
        ]
        + ([] if start is None else [whole]),
        out_specs=[whole] + grad_specs,
        out_shape=[jax.ShapeDtypeStruct((rows, wide), F32)] + grad_types,
        scratch_shapes=[pltpu.VMEM((rows, tile), BF16)],
        compiler_params=kernel_limits(60),
        cost_estimate=estimate(7 * rows * wide * width, 6 * wide * width),
        name="mlp_back",
    )(me, grad, field, slope, w_in, w_out, *([] if start is None else [start]))
    return (outs[0], outs[1:])


def gate_kernel(share, me_ref, live_ref, mixed_ref, gv_ref, w_ref, gated_ref, dmix_ref, *grads):
    live = live_ref[0].astype(F32)
    mixed = mixed_ref[...]
    mixed_low = mixed.astype(BF16)
    wide = mixed.shape[1]
    wi, wo = (w_ref[:, :wide], w_ref[:, wide:])
    act, slope = gelu_pair(dot(mixed_low, wi, NN))
    act = act.astype(BF16)
    gate = jnp.tanh(dot(act, wo, NN))
    gated_ref[...] = gate * mixed
    grad = live * gv_ref[...].astype(F32)
    logit = (grad * mixed * (1.0 - gate * gate)).astype(BF16)
    low = (dot(logit, wo, NT) * slope).astype(BF16)
    for place, (left, right) in enumerate(((mixed_low, low), (act, logit))):
        lanes = slice(place * wide, (place + 1) * wide)
        if share:
            spot = (slice(None), slice(None), lanes)
            store_shares(dot(left, right, TN), share, me_ref[0] % 2 == 0, *grads, spot)
        else:
            grads[0][:, lanes] = dot(left, right, TN).astype(BF16)
    dmix_ref[...] = grad * gate + dot(low, wi, NT)


def gate_both(mixed, grad, live, me, weights, devices):
    rows, wide = mixed.shape
    share = wide // devices
    grad_types = [share_type(devices, share, 2 * wide)] * 2
    if share % 16:
        share = 0
        grad_types = [jax.ShapeDtypeStruct((wide, 2 * wide), BF16)]
    return pl.pallas_call(
        functools.partial(gate_kernel, share),
        in_specs=[SCALARS, SCALARS, LOCAL, LOCAL, LOCAL],
        out_specs=[LOCAL] * (2 + len(grad_types)),
        out_shape=[jax.ShapeDtypeStruct((rows, wide), F32)] * 2 + grad_types,
        compiler_params=kernel_limits(60),
        cost_estimate=estimate(20 * rows * wide * wide, 30 * rows * wide),
        name="gate_both",
    )(me, live, mixed, grad, weights)


def bit_pairs(devices, bit):
    return [(index, index ^ (1 << bit)) for index in range(devices)]


def own_bit(bit):
    return (lax.axis_index("fsdp") >> bit) & 1


def gather_small(block, devices):
    gathered = block[None]
    for bit in range(devices.bit_length() - 1):
        other = lax.ppermute(gathered, "fsdp", bit_pairs(devices, bit))
        high = own_bit(bit) == 1
        gathered = jnp.where(
            high,
            jnp.concatenate((other, gathered), axis=0),
            jnp.concatenate((gathered, other), axis=0),
        )
    return gathered


def after(values, earlier):
    if not earlier:
        return list(values)
    return list(lax.optimization_barrier(tuple(values) + tuple(earlier))[: len(values)])


def swap(block, bits, devices):
    mask = sum(1 << bit for bit in bits)
    return lax.ppermute(block, "fsdp", [(index, index ^ mask) for index in range(devices)])


def axis_bits(devices):
    bits = devices.bit_length() - 1
    if bits == 5:
        return ((1,), (2,), (3, 4))
    span = (bits - 1 + 2) // 3
    places = tuple(range(1, bits))
    return (places[:span], places[span : 2 * span], places[2 * span :])


def subsets(bits):
    found = [()]
    for bit in bits:
        found = found + [each + (bit,) for each in found]
    return found


def mask_of(bits):
    return sum(1 << bit for bit in bits)


class Gatherer:
    def __init__(self, devices):
        self.devices = devices
        self.x_bits, self.y_bits, self.z_bits = axis_bits(devices)
        self.last = []
        self.ends = []

    def doubled(self, field, slots, bits):
        for bit in bits:
            other = swap(field, (bit,), self.devices)
            field = jnp.concatenate((field, other), axis=0)
            slots = slots + [slot ^ (1 << bit) for slot in slots]
        return (field, slots)

    def group(self, block, begin, end, middle):
        rows = block.shape[0]
        (own,) = after((block[None, :, begin:end],), self.last)
        fields, slots = ([own], [0])
        for bits in subsets(self.z_bits)[1:]:
            fields.append(swap(own, bits, self.devices))
            slots.append(mask_of(bits))
        plan, sources, firsts, seconds = ([], [], [], [])
        for first, last, left, right in (
            (self.x_bits, self.y_bits, begin, middle),
            (self.y_bits, self.x_bits, middle, end),
        ):
            field = jnp.concatenate(
                [each[:, :, left - begin : right - begin] for each in fields], axis=0
            )
            (field,) = after((field,), self.ends)
            firsts.append((*self.doubled(field, slots, first), last, left, right))
        self.last = [each[0] for each in firsts]
        self.ends = []
        for field, its_slots, last, left, right in firsts:
            held = [(field, its_slots)]
            for bit in last + (0,):
                if bit == 0:
                    self.ends += [part for part, _ in held[1:]]
                held = held + [
                    (swap(part, (bit,), self.devices), [slot ^ (1 << bit) for slot in part_slots])
                    for part, part_slots in held
                ]
            for part, part_slots in held:
                sources.append(part)
                plan.append((tuple(part_slots), rows, 0, left, right))
        return (plan, sources)

    def weight(self, block, groups):
        plan, sources = ([], [])
        rows = block.shape[0]
        if rows % 16:
            whole = lax.all_gather(block, "fsdp", axis=0, tiled=True)[None]
            plan = [((None,), rows * self.devices, begin, begin, end) for begin, _, end in groups]
            return (plan, [whole] * len(groups))
        for begin, middle, end in groups:
            more_plan, more_sources = self.group(block, begin, end, middle)
            plan += more_plan
            sources += more_sources
        return (plan, sources)


def take(field, axis, place):
    return lax.dynamic_index_in_dim(field, place, axis, keepdims=False)


def halved(field, held, bit, devices):
    axis = held.index(bit)
    mine = own_bit(bit)
    arrived = swap(take(field, axis, 1 - mine), (bit,), devices)
    return (take(field, axis, mine) + arrived, held[:axis] + held[axis + 1 :])


def combine_kernel(parts, stacked, me_ref, *refs):
    count = 4 * sum(len(widths) for widths in parts)
    blocks, outs = (refs[:count], refs[count:])
    sums = []
    for widths in parts:
        kept, sent = ([], [])
        for _ in widths:
            (a, b, c, d), blocks = (blocks[:4], blocks[4:])
            kept.append((a[0].astype(F32) + b[0].astype(F32)).astype(BF16))
            sent.append((c[0].astype(F32) + d[0].astype(F32)).astype(BF16))
        sums.append((kept, sent))
    if not stacked:
        for place, pair in enumerate(sums):
            for out_ref, values in zip(outs[2 * place : 2 * place + 2], pair):
                begin = 0
                for value in values:
                    out_ref[0, :, begin : begin + value.shape[1]] = value
                    begin += value.shape[1]
        return
    for which, out_ref in enumerate(outs):
        line = 0
        for pair in sums:
            (value,) = pair[which]
            rows, columns = value.shape
            for begin in range(0, columns, stacked):
                out_ref[0, line : line + rows, :] = value[:, begin : begin + stacked]
                line += rows


def combine(me, parts, stacked):
    def spec(rows, width, bit, after_it, other, begin):
        def index(slot, me_ref):
            mine = (me_ref[0] >> bit) & 1
            mine = 1 - mine if other else mine
            return ((slot // after_it * 2 + mine) * after_it + slot % after_it, 0, begin // width)

        return pl.BlockSpec((1, rows, width), index)

    in_specs, operands, widths, shapes, moved = ([], [], [], [], 0)
    for bit, before, after_it, segments in parts:
        slots = before * after_it
        for kept, arrived, begin, width in segments:
            rows = kept.shape[1]
            for other in (False, True):
                in_specs += [spec(rows, width, bit, after_it, other, begin)] * 2
                operands += [kept, arrived]
            moved += 6 * slots * rows * width
        widths.append([segment[3] for segment in segments])
        shapes.append((rows, sum(widths[-1])))
    if stacked:
        total = sum(rows * columns // stacked for rows, columns in shapes)
        shapes = [(total, stacked)]
    out_specs, out_types = ([], [])
    for shape in shapes:
        out_specs += [pl.BlockSpec((1,) + shape, lambda slot, me_ref: (slot, 0, 0))] * 2
        out_types += [jax.ShapeDtypeStruct((slots,) + shape, BF16)] * 2
    outs = pl.pallas_call(
        functools.partial(combine_kernel, widths, stacked),
        grid_spec=pltpu.PrefetchScalarGridSpec(
            num_scalar_prefetch=1,
            grid=(slots,),
            in_specs=in_specs,
            out_specs=out_specs,
        ),
        out_shape=out_types,
        compiler_params=kernel_limits(48),
        cost_estimate=estimate(moved, 2 * moved),
        name="combine",
    )(me, *operands)
    return list(zip(outs[::2], outs[1::2]))


class Scatterer:
    def __init__(self, devices, me, gradients, parts, early=False):
        x_bits, y_bits, z_bits = axis_bits(devices)
        self.me = me
        self.bits = devices.bit_length() - 1
        self.orders = (y_bits + x_bits + z_bits, x_bits + y_bits + z_bits)
        self.split = 0 if early else len(x_bits + y_bits)
        if early:
            self.orders = (self.orders[0],) * 2
        self.parts = parts
        self.shapes = [
            (gradients[part[0][0]][0].shape[1], sum(width for _, _, width in part)) for part in parts
        ]
        self.width = min(columns for _, columns in self.shapes)
        self.stage = -1
        self.kept = [mine for mine, _ in gradients]
        self.sends = [(theirs, 0) for _, theirs in gradients]
        self.result = None

    def receive(self, arrived):
        pairs = list(zip(self.kept, arrived))
        self.stage += 1
        if self.stage == self.bits - 1:
            total = pairs[0][0][0].astype(F32) + pairs[0][1][0].astype(F32)
            self.sends, self.result = ([], [])
            line = 0
            for rows, columns in self.shapes:
                pieces = []
                for _ in range(columns // self.width):
                    pieces.append(total[line : line + rows])
                    line += rows
                self.result.append(jnp.concatenate(pieces, axis=1))
            return
        if self.stage == 0:
            segments = [
                [(*pairs[place], begin, width) for place, begin, width in part]
                for part in self.parts
            ]
            self.held = [list(range(self.bits - 1, 0, -1))] * 2
        else:
            segments = [[(*pair, 0, pair[0].shape[2])] for pair in pairs]
        parts, helds = ([], [])
        for order, held, its_segments in zip(self.orders, self.held, segments):
            bit = order[self.stage]
            axis = held.index(bit)
            parts.append((bit, 2**axis, 2 ** (len(held) - axis - 1), its_segments))
            helds.append(held[:axis] + held[axis + 1 :])
        self.held = helds
        sums = combine(self.me, parts, self.width if self.stage == self.split else 0)
        self.kept = [kept for kept, _ in sums]
        self.sends = [(sent, part[0]) for (_, sent), part in zip(sums, parts)]


class Ticks:
    def __init__(self):
        self.before = []

    def run(self, groups, value, work):
        groups = [group for group in groups if group.result is None]
        sends = [each for group in groups for each in group.sends]
        value, *blocks = after([value] + [block for block, _ in sends], self.before)
        devices = lax.axis_size("fsdp")
        arrived = [swap(block, (bit,), devices) for block, (_, bit) in zip(blocks, sends)]
        outs = jax.tree.leaves(work(value))
        done = after(outs + arrived, [])
        if len(done) > 1:
            done = list(lax.optimization_barrier(tuple(done)))
        outs, arrived = (done[: len(outs)], done[len(outs) :])
        begin = 0
        for group in groups:
            count = len(group.sends)
            group.receive(arrived[begin : begin + count])
            begin += count
        self.before = outs[:1]
        return outs

    def finish(self, groups):
        while any(group.result is None for group in groups):
            self.run(groups, jnp.zeros((), F32), lambda value: value)


def halves(gradient, devices):
    pairs = gradient.reshape((devices // 2, 2) + gradient.shape[1:])
    mine = own_bit(0)
    return (take(pairs, 1, mine), take(pairs, 1, 1 - mine))


def shards(
    x_vit,
    x_hires,
    image_live,
    grad_vit,
    grad_hires,
    gain_one,
    w_qkv,
    w_out,
    gain_two,
    w_up,
    w_down,
    conv_seven,
    gain_three,
    w_expand,
    w_shrink,
    layer_scale,
    w_adapt,
    conv_three,
    w_gate_in,
    w_gate_out,
):
    devices = lax.axis_size("fsdp")
    edge_c, edge_d = (gain_three.shape[0], gain_one.shape[0])
    small = jnp.concatenate(
        (
            conv_seven.reshape(-1),
            gain_three,
            layer_scale,
            conv_three.reshape(-1),
            gain_one,
            gain_two,
        )
    )
    small_all = gather_small(small, devices)
    marks = [0]
    for length in (KS * KS * edge_c, edge_c, edge_c, KA * KA * edge_d, edge_d, edge_d):
        marks.append(marks[-1] + length)
    small_parts = [small_all[:, marks[place] : marks[place + 1]] for place in range(6)]
    seven_taps = small_parts[0].reshape(devices, KS * KS, edge_c).swapaxes(0, 1).reshape(KS * KS, C)
    three_taps = small_parts[3].reshape(devices, KA * KA, edge_d).swapaxes(0, 1).reshape(KA * KA, D)
    gain_c, scale_c = (small_parts[1].reshape(C).astype(F32), small_parts[2].reshape(C).astype(F32))
    gain_a, gain_b = (small_parts[4].reshape(D).astype(F32), small_parts[5].reshape(D).astype(F32))

    me = lax.axis_index("fsdp").astype(jnp.int32).reshape(1)
    def gathered(block):
        return lax.all_gather(block, "fsdp", axis=0, tiled=True)

    live = image_live.astype(F32)
    vit_all = gathered(jnp.concatenate((w_qkv, w_out), axis=1))
    qkv_all, out_all = (vit_all[:, : 3 * D], vit_all[:, 3 * D :])
    gates_all = gathered(jnp.concatenate((w_gate_in, w_gate_out), axis=1))
    adapt_all = gathered(w_adapt)
    tile = D
    tiles = w_expand.shape[1] // tile
    gatherer = Gatherer(devices)
    expand_pieces = gatherer.weight(w_expand, [(0, C, 2 * C)])
    conved = depthwise(after((x_hires,), gatherer.last)[0], seven_taps, KS, GRID_HR)
    normed_c, inverse_c = norm_rows(conved, 1e-06)
    normed_c_low = (normed_c * gain_c).astype(BF16)
    gatherer.ends.append(normed_c_low)
    more_pieces = gatherer.weight(w_expand, [(2 * C, 3 * C, 4 * C)])
    expand_pieces = tuple(one + two for one, two in zip(expand_pieces, more_pieces))

    def attention(x_vit):
        patch_in = x_vit.astype(F32)
        normed_a, inverse_a = norm_rows(patch_in, 1e-05)
        normed_a_low = (normed_a * gain_a).astype(BF16)
        qkv_low = dot(normed_a_low, qkv_all, NN).astype(BF16)
        attended_low = attend(qkv_low)
        resid_one = patch_in + dot(attended_low, out_all, NN)
        normed_b, inverse_b = norm_rows(resid_one, 1e-05)
        normed_b_low = (normed_b * gain_b).astype(BF16)
        return (
            normed_b_low, qkv_low, attended_low, resid_one, normed_a, inverse_a, normed_b, inverse_b, normed_a_low
        )

    (
        normed_b_low, qkv_low, attended_low, resid_one, normed_a, inverse_a, normed_b, inverse_b, normed_a_low
    ) = attention(after((x_vit,), gatherer.last)[0])
    gatherer.ends.append(normed_b_low)
    shrink_pieces = gatherer.weight(w_shrink, [(0, C // 4, C // 2)])
    field_c = after((normed_c_low,), gatherer.last)[0]
    activated, slope, expand_all = expand(
        field_c, expand_pieces, me, w_expand.shape[1], tile, 256
    )
    gatherer.ends.append(activated)
    more_pieces = gatherer.weight(w_shrink, [(C // 2, 3 * C // 4, C)])
    shrink_pieces = tuple(one + two for one, two in zip(shrink_pieces, more_pieces))
    up_all = gathered(after((w_up,), gatherer.last)[0])
    down_all = gathered(after((w_down,), gatherer.last)[0])

    def shares(gradient):
        return gradient.reshape(devices, gradient.shape[0] // devices, gradient.shape[1])

    def split(gradient):
        if len(gradient) == 2:
            return tuple(gradient)
        return halves(shares(gradient[0]), devices)

    ticks = Ticks()

    shrunk, hires_low, hires_next, shrink_all = ticks.run(
        [],
        activated,
        lambda act: shrink(
            act, x_hires, scale_c.reshape(1, C), image_live, shrink_pieces, me, C // 2
        ),
    )

    table = pool_table(GRID_HR, GRID_LR)
    pool = jnp.einsum("ia,jb->ijab", table, table).reshape(GRID_LR**2, GRID_HR**2).astype(BF16)

    def adapter(hires_low):
        pooled_low = dot(pool, hires_low, NN).astype(BF16)
        adapted = dot(pooled_low, adapt_all, NN)
        mixed = depthwise(adapted, three_taps, KA, GRID_LR)
        gated, grad_mixed, *d_gates = gate_both(
            mixed, grad_vit, image_live, me, gates_all, devices
        )
        return (grad_mixed, gated, pooled_low, adapted, *d_gates)

    grad_mixed, gated, pooled_low, adapted, *d_gates = ticks.run(
        [], hires_low, adapter
    )

    def adapter_back(grad_mixed):
        grad_adapted_low, d_conv_three = depthwise_back(
            grad_mixed, adapted, jnp.zeros(adapted.shape, BF16), three_taps, KA, GRID_LR, 0, D
        )
        d_adapt = outer_sum(pooled_low, grad_adapted_low, me, edge_c)
        grad_pooled_low = dot(grad_adapted_low, adapt_all, NT).astype(BF16)
        grad_hires_out = live * grad_hires.astype(F32) + dot(pool, grad_pooled_low, TN)
        d_layer_scale = jnp.sum(grad_hires_out * shrunk, axis=0)
        grad_shrunk_low = (grad_hires_out * scale_c).astype(BF16)
        return (grad_shrunk_low, d_layer_scale, grad_hires_out, d_conv_three, *d_adapt)

    grad_shrunk_low, d_layer_scale, grad_hires_out, d_conv_three, *d_adapt = ticks.run(
        [], grad_mixed, adapter_back
    )
    sum_square = Scatterer(
        devices,
        me,
        [split(d_gates), split(d_adapt)],
        [[(0, 0, 2 * D)], [(1, 0, D)]],
        early=True,
    )

    outs = ticks.run(
        [sum_square],
        grad_shrunk_low,
        lambda grad: outer_sum(activated, grad, me, w_shrink.shape[0]),
    )
    sum_shrink = Scatterer(
        devices, me, [tuple(outs)], [[(0, 0, C // 2)], [(0, C // 2, C // 2)]]
    )
    sums_expand = []

    def network_back(groups, grad_c, part):
        value = grad_shrunk_low if grad_c is None else grad_c
        sums, *d_part = ticks.run(
            groups,
            value,
            lambda value: mlp_back(
                value if grad_c is None else grad_shrunk_low,
                normed_c_low,
                slope,
                expand_all,
                shrink_all,
                None if grad_c is None else value,
                me,
                devices,
                tile,
                512,
                part * tiles // 2,
                (part + 1) * tiles // 2,
            ),
        )
        width = w_expand.shape[1] // 4
        sums_expand.append(
            Scatterer(devices, me, [split(d_part)], [[(0, 0, width)], [(0, width, width)]])
        )
        return sums

    grad_c = network_back([sum_square, sum_shrink], None, 0)

    grad_joined_low = (grad_vit.astype(F32) * live).astype(BF16)

    def network_both(field):
        mlp_out, grad_b, d_up, d_down = mlp_both(
            grad_joined_low, field, up_all, down_all, me, devices, D
        )
        return (mlp_out, grad_b, *d_up, *d_down)

    mlp_out, grad_b, *d_hidden = ticks.run(
        [sum_shrink, sums_expand[0]], normed_b_low, network_both
    )
    sum_mlp = Scatterer(
        devices,
        me,
        [split(d_hidden[:-2]), split(d_hidden[-2:])],
        [[(0, 0, w_up.shape[1])], [(1, 0, D)]],
    )
    joined = (live * (resid_one + mlp_out + gated)).astype(BF16)
    d_gain_two = jnp.sum(grad_b * normed_b, axis=0)
    grad_first = grad_joined_low.astype(F32) + norm_back(grad_b * gain_b, normed_b, inverse_b)
    grad_c = network_back([sum_shrink, sum_mlp, sum_square], grad_c, 1)

    def attention_back(grad_first):
        grad_first_low = grad_first.astype(BF16)
        grad_att_low = dot(grad_first_low, out_all, NT).astype(BF16)
        d_out = outer_sum(attended_low, grad_first_low, me, edge_d)
        return (*attend_back(qkv_low, grad_att_low), *d_out)

    *grads_three, out_mine, out_theirs = ticks.run(
        [sum_mlp, sum_shrink, sums_expand[1], sum_square], grad_first, attention_back
    )

    def projection_back(grad_queries):
        grad_qkv_low = jnp.concatenate((grad_queries, *grads_three[1:]), axis=1)
        d_qkv = outer_sum(normed_a_low, grad_qkv_low, me, edge_d)
        grad_a = dot(grad_qkv_low, qkv_all, NT)
        d_gain_one = jnp.sum(grad_a * normed_a, axis=0)
        grad_patches = grad_first + norm_back(grad_a * gain_a, normed_a, inverse_a)
        return (grad_patches, d_gain_one, *d_qkv)

    grad_patches, d_gain_one, *d_qkv = ticks.run(
        [sums_expand[0], sum_mlp, sum_shrink], grads_three[0], projection_back
    )
    sum_attention = Scatterer(
        devices,
        me,
        [tuple(d_qkv), (out_mine, out_theirs)],
        [[(0, 0, 2 * D)], [(0, 2 * D, D), (1, 0, D)]],
    )

    d_gain_three = jnp.sum(grad_c * normed_c, axis=0)
    grad_conved = norm_back(grad_c * gain_c, normed_c, inverse_c)
    grad_hires_in = grad_hires_out
    pieces_seven = []
    width = C // 3
    beside = (
        [sums_expand[1], sums_expand[0], sum_mlp],
        [sum_attention, sums_expand[1], sum_mlp],
        [sum_attention] + sums_expand,
    )
    for part in range(3):
        grad_hires_in, taps_part = ticks.run(
            beside[part],
            grad_hires_in,
            lambda base, part=part: depthwise_back(
                grad_conved,
                x_hires,
                base,
                seven_taps,
                KS,
                GRID_HR,
                part * width,
                (part + 1) * width,
            ),
        )
        pieces_seven.append(taps_part)
    d_conv_seven = jnp.concatenate(pieces_seven, axis=1)
    ticks.run([sum_attention, sum_square] + sums_expand, jnp.zeros((), F32), lambda value: value)
    small_grads = jnp.concatenate(
        (
            d_conv_seven.reshape(KS * KS, devices, edge_c).swapaxes(0, 1).reshape(devices, -1),
            d_gain_three.reshape(devices, edge_c),
            d_layer_scale.reshape(devices, edge_c),
            d_conv_three.reshape(KA * KA, devices, edge_d).swapaxes(0, 1).reshape(devices, -1),
            d_gain_one.reshape(devices, edge_d),
            d_gain_two.reshape(devices, edge_d),
        ),
        axis=1,
    )
    small_grads = after((small_grads,), ticks.before)[0]
    ticks.finish([sum_attention, sum_mlp, sum_shrink, sum_square] + sums_expand)
    g_up, g_down = sum_mlp.result
    g_attention = jnp.concatenate(sum_attention.result, axis=1)
    g_gates, g_adapt = sum_square.result
    g_shrink = jnp.concatenate(sum_shrink.result, axis=1)
    g_expand = jnp.concatenate([part for each in sums_expand for part in each.result], axis=1)
    small_sums = small_grads.reshape((2,) * (devices.bit_length() - 1) + small_grads.shape[1:])
    held = list(range(devices.bit_length() - 2, -1, -1))
    for bit in range(devices.bit_length() - 1):
        small_sums, held = halved(small_sums, held, bit, devices)
    small_outs = [small_sums[marks[place] : marks[place + 1]] for place in range(6)]
    return (
        joined,
        hires_next,
        grad_patches,
        grad_hires_in,
        small_outs[4],
        g_attention[:, : 3 * D],
        g_attention[:, 3 * D :],
        small_outs[5],
        g_up,
        g_down,
        small_outs[0].reshape(KS * KS, edge_c),
        small_outs[1],
        g_expand,
        g_shrink,
        small_outs[2],
        g_adapt,
        small_outs[3].reshape(KA * KA, edge_d),
        g_gates[:, :D],
        g_gates[:, D:],
    )


def solution(mesh):
    in_specs = (
        P("fsdp", None),
        P("fsdp", None),
        P("fsdp"),
        P("fsdp", None),
        P("fsdp", None),
        P("fsdp"),
        P("fsdp", None),
        P("fsdp", None),
        P("fsdp"),
        P("fsdp", None),
        P("fsdp", None),
        P(None, "fsdp"),
        P("fsdp"),
        P("fsdp", None),
        P("fsdp", None),
        P("fsdp"),
        P("fsdp", None),
        P(None, "fsdp"),
        P("fsdp", None),
        P("fsdp", None),
    )
    out_specs = (
        P("fsdp", None),
        P("fsdp", None),
        P("fsdp", None),
        P("fsdp", None),
        P("fsdp"),
        P("fsdp", None),
        P("fsdp", None),
        P("fsdp"),
        P("fsdp", None),
        P("fsdp", None),
        P(None, "fsdp"),
        P("fsdp"),
        P("fsdp", None),
        P("fsdp", None),
        P("fsdp"),
        P("fsdp", None),
        P(None, "fsdp"),
        P("fsdp", None),
        P("fsdp", None),
    )
    return jax.shard_map(shards, mesh=mesh, in_specs=in_specs, out_specs=out_specs, check_vma=False)
```

```python
import functools
import math

import jax
import jax.numpy as jnp
import numpy as np
from jax import lax
from jax.experimental import pallas as pl
from jax.experimental.pallas import tpu as pltpu
from jax.sharding import PartitionSpec as P

D = 1024
HEAD_DIM = 64
C = 1536
KS = 7
KA = 3
GRID_LR = 24
GRID_HR = 32
LANES = 128
GROUP = 8
NN = ((1,), (0,))
NT = ((1,), (1,))
TN = ((0,), (0,))
BF16 = jnp.bfloat16
F32 = jnp.float32


def dot(left, right, dims):
    return lax.dot_general(left, right, (dims, ((), ())), preferred_element_type=F32)


def kernel_limits(mebibytes):
    return pltpu.CompilerParams(vmem_limit_bytes=mebibytes * 2**20)


def estimate(flops, moved):
    return pl.CostEstimate(flops=flops, bytes_accessed=moved, transcendentals=0)


def norm_rows(values, epsilon):
    average = jnp.mean(values, axis=-1, keepdims=True)
    centred = values - average
    spread = jnp.mean(centred * centred, axis=-1, keepdims=True)
    inverse = lax.rsqrt(spread + epsilon)
    return (centred * inverse, inverse)


def norm_back(grad_normed, normed, inverse):
    first_mean = jnp.mean(grad_normed, axis=-1, keepdims=True)
    second_mean = jnp.mean(grad_normed * normed, axis=-1, keepdims=True)
    return inverse * (grad_normed - first_mean - normed * second_mean)


def gelu_pair(values):
    cdf = 0.5 * (1.0 + lax.erf(values * (1.0 / math.sqrt(2.0))))
    density = jnp.exp(-0.5 * values * values) * (1.0 / math.sqrt(2.0 * math.pi))
    return (values * cdf, cdf + values * density)


def pool_matrix(fine_cells, coarse_cells):
    coarse_index = np.arange(coarse_cells)[:, None]
    fine_index = np.arange(fine_cells)[None, :]
    window_start = coarse_index * fine_cells // coarse_cells
    window_end = ((coarse_index + 1) * fine_cells + coarse_cells - 1) // coarse_cells
    inside = ((fine_index >= window_start) & (fine_index < window_end)).astype(np.float32)
    table = inside / np.sum(inside, axis=1, keepdims=True)
    return jnp.asarray(np.kron(table, table), BF16)


def fill_shifted(shifted, field, width, edge):
    reach = width // 2
    cells, lanes = field.shape
    column = lax.broadcasted_iota(jnp.int32, (cells, lanes), 0) % edge
    for step in range(width):
        offset = step - reach
        moved = field
        if offset != 0:
            moved = pltpu.roll(field, (-offset) % cells, 0)
            inside = (column + offset >= 0) & (column + offset < edge)
            moved = jnp.where(inside, moved, 0.0)
        shifted[step, reach : reach + edge] = moved.reshape(edge, edge, lanes)


def clear_edges(shifted, width, edge):
    reach = width // 2
    border = jnp.zeros((width, reach) + shifted.shape[2:], F32)
    shifted[:, 0:reach] = border
    shifted[:, reach + edge :] = border


def depthwise_kernel(width, edge, field_ref, taps_ref, out_ref, shifted, wide):
    @pl.when(pl.program_id(0) == 0)
    def _():
        clear_edges(shifted, width, edge)

    fill_shifted(shifted, field_ref[...].astype(F32), width, edge)
    wide[...] = jnp.broadcast_to(taps_ref[...].astype(F32)[:, None, :], wide.shape)
    strips = edge // 8

    def body(index, carry):
        base = (index // strips) * GROUP
        column = pl.multiple_of((index % strips) * 8, 8)
        sums = [jnp.zeros((8, LANES), F32)] * GROUP
        for step in range(width):
            taps = [wide[tap * width + step] for tap in range(width)]
            for row in range(GROUP + width - 1):
                value = shifted[step, base + row, pl.ds(column, 8), :]
                for place in range(GROUP):
                    if 0 <= row - place < width:
                        sums[place] = sums[place] + value * taps[row - place]
        for place in range(GROUP):
            start = pl.multiple_of((base + place) * edge + column, 8)
            out_ref[pl.ds(start, 8), :] = sums[place]
        return carry

    lax.fori_loop(0, (edge // GROUP) * strips, body, 0)


def depthwise(field, taps, width, edge):
    cells, channels = field.shape
    return pl.pallas_call(
        functools.partial(depthwise_kernel, width, edge),
        grid=(channels // LANES,),
        in_specs=[
            pl.BlockSpec((cells, LANES), lambda i: (0, i)),
            pl.BlockSpec((width * width, LANES), lambda i: (0, i)),
        ],
        out_specs=pl.BlockSpec((cells, LANES), lambda i: (0, i)),
        out_shape=jax.ShapeDtypeStruct((cells, channels), F32),
        scratch_shapes=[
            pltpu.VMEM((width, edge + width - 1, edge, LANES), F32),
            pltpu.VMEM((width * width, 8, LANES), F32),
        ],
        compiler_params=kernel_limits(32),
        cost_estimate=estimate(600 * width * width * cells * channels, 8 * cells * channels),
        name="depthwise",
    )(field, taps)


def depthwise_back_kernel(
    width, edge, grad_ref, field_ref, base_ref, taps_ref, out_ref, tap_out_ref, shifted, wide, cells_ref, sums_ref
):
    @pl.when(pl.program_id(0) == 0)
    def _():
        clear_edges(shifted, width, edge)

    fill_shifted(shifted, grad_ref[...], width, edge)
    cells_ref[...] = field_ref[...].astype(F32)
    sums_ref[...] = base_ref[...].astype(F32)
    wide[...] = jnp.broadcast_to(taps_ref[...].astype(F32)[:, None, :], wide.shape)
    strips = edge // 8
    last = width - 1

    for step in range(width):
        taps = [wide[(last - tap) * width + (last - step)] for tap in range(width)]

        def body(index, tap_sums):
            tap_sums = list(tap_sums)
            base = (index // strips) * GROUP
            column = pl.multiple_of((index % strips) * 8, 8)
            spots = [
                pl.ds(pl.multiple_of((base + place) * edge + column, 8), 8)
                for place in range(GROUP)
            ]
            sums = [sums_ref[spot, :] for spot in spots]
            cells = [cells_ref[spot, :] for spot in spots]
            for row in range(GROUP + width - 1):
                value = shifted[step, base + row, pl.ds(column, 8), :]
                for place in range(GROUP):
                    tap = row - place
                    if 0 <= tap < width:
                        sums[place] = sums[place] + value * taps[tap]
                        tap_sums[tap] = tap_sums[tap] + value * cells[place]
            for place in range(GROUP):
                sums_ref[spots[place], :] = sums[place]
            return tuple(tap_sums)

        tap_sums = lax.fori_loop(
            0, (edge // GROUP) * strips, body, (jnp.zeros((8, LANES), F32),) * width
        )
        for tap in range(width):
            spot = (last - tap) * width + (last - step)
            tap_out_ref[spot : spot + 1, :] = jnp.sum(tap_sums[tap], axis=0, keepdims=True)
    out_ref[...] = sums_ref[...].astype(out_ref.dtype)


def depthwise_back(grad, field, base, taps, width, edge, first, last):
    cells, channels = field.shape
    skip = first // LANES
    full = pl.BlockSpec((cells, LANES), lambda i: (0, i + skip))
    small = pl.BlockSpec((width * width, LANES), lambda i: (0, i + skip))
    return pl.pallas_call(
        functools.partial(depthwise_back_kernel, width, edge),
        grid=((last - first) // LANES,),
        in_specs=[full, full, full, small],
        out_specs=[full, pl.BlockSpec((width * width, LANES), lambda i: (0, i))],
        out_shape=[
            jax.ShapeDtypeStruct((cells, channels), base.dtype),
            jax.ShapeDtypeStruct((width * width, last - first), F32),
        ],
        scratch_shapes=[
            pltpu.VMEM((width, edge + width - 1, edge, LANES), F32),
            pltpu.VMEM((width * width, 8, LANES), F32),
            pltpu.VMEM((cells, LANES), F32),
            pltpu.VMEM((cells, LANES), F32),
        ],
        input_output_aliases={2: 0},
        compiler_params=kernel_limits(32),
        cost_estimate=estimate(
            1200 * width * width * cells * (last - first), 14 * cells * (last - first)
        ),
        name="depthwise_back",
    )(grad, field, base, taps)


def softmax_rows(query, key):
    scores = dot(query, key, NT) * HEAD_DIM ** (-0.5)
    raised = jnp.exp(scores - jnp.max(scores, axis=-1, keepdims=True))
    return raised * (1.0 / jnp.sum(raised, axis=-1, keepdims=True))


def attend_kernel(q_ref, k_ref, v_ref, out_ref):
    outs = []
    for head in range(out_ref.shape[1] // HEAD_DIM):
        lanes = slice(head * HEAD_DIM, (head + 1) * HEAD_DIM)
        probs = softmax_rows(q_ref[:, lanes], k_ref[:, lanes]).astype(BF16)
        outs.append(dot(probs, v_ref[:, lanes], NN))
    out_ref[...] = jnp.concatenate(outs, axis=1).astype(BF16)


def attend(qkv, width=256):
    rows = qkv.shape[0]
    steps = D // width

    def spec(part):
        return pl.BlockSpec((rows, width), lambda i: (0, i + part * steps))

    return pl.pallas_call(
        attend_kernel,
        grid=(steps,),
        in_specs=[spec(0), spec(1), spec(2)],
        out_specs=spec(0),
        out_shape=jax.ShapeDtypeStruct((rows, D), BF16),
        compiler_params=kernel_limits(48),
        cost_estimate=estimate(40 * rows * rows * D, 8 * rows * D),
        name="attend",
    )(qkv, qkv, qkv)


def attend_back_kernel(q_ref, k_ref, v_ref, g_ref, dq_ref, dk_ref, dv_ref):
    scale = HEAD_DIM ** (-0.5)
    dqs, dks, dvs = ([], [], [])
    for head in range(dq_ref.shape[1] // HEAD_DIM):
        lanes = slice(head * HEAD_DIM, (head + 1) * HEAD_DIM)
        query, key, value, grad = (q_ref[:, lanes], k_ref[:, lanes], v_ref[:, lanes], g_ref[:, lanes])
        probs = softmax_rows(query, key)
        grad_probs = dot(grad, value, NT)
        dvs.append(dot(probs.astype(BF16), grad, TN))
        total = jnp.sum(probs * grad_probs, axis=-1, keepdims=True)
        low = (probs * (grad_probs - total)).astype(BF16)
        dqs.append(dot(low, key, NN) * scale)
        dks.append(dot(low, query, TN) * scale)
    dq_ref[...] = jnp.concatenate(dqs, axis=1).astype(BF16)
    dk_ref[...] = jnp.concatenate(dks, axis=1).astype(BF16)
    dv_ref[...] = jnp.concatenate(dvs, axis=1).astype(BF16)


def attend_back(qkv, grad, width=256):
    rows = qkv.shape[0]
    steps = D // width

    def spec(part):
        return pl.BlockSpec((rows, width), lambda i: (0, i + part * steps))

    return pl.pallas_call(
        attend_back_kernel,
        grid=(steps,),
        in_specs=[spec(0), spec(1), spec(2), spec(0)],
        out_specs=[spec(0)] * 3,
        out_shape=[jax.ShapeDtypeStruct((rows, D), BF16)] * 3,
        compiler_params=kernel_limits(48),
        cost_estimate=estimate(70 * rows * rows * D, 14 * rows * D),
        name="attend_back",
    )(qkv, qkv, qkv, grad)


def start_copies(plan, me, sources, target, semaphore, first=0, last=None):
    for source, (slots, rows, offset, begin, end) in zip(sources, plan):
        left, right = (max(begin, first), end if last is None else min(end, last))
        if left >= right:
            continue
        for place, slot in enumerate(slots):
            line = 0 if slot is None else pl.multiple_of((me ^ slot) * rows, rows)
            pltpu.make_async_copy(
                source.at[place, :, pl.ds(left - begin + offset, right - left)],
                target.at[pl.ds(line, rows), pl.ds(left - first, right - left)],
                semaphore,
            ).start()


def store_shares(value, rows, even, mine_ref, theirs_ref, lines=slice(None)):
    low = value.astype(BF16).reshape(-1, 2, rows, value.shape[-1])

    @pl.when(even)
    def _():
        mine_ref[lines] = low[:, 0]
        theirs_ref[lines] = low[:, 1]

    @pl.when(jnp.logical_not(even))
    def _():
        mine_ref[lines] = low[:, 1]
        theirs_ref[lines] = low[:, 0]


def share_type(devices, rows, columns):
    return jax.ShapeDtypeStruct((devices // 2, rows, columns), BF16)


SCALARS = pl.BlockSpec(memory_space=pltpu.SMEM)
ANYWHERE = pl.BlockSpec(memory_space=pl.ANY)
LOCAL = pl.BlockSpec(memory_space=pltpu.VMEM)


def mlp_both_kernel(shares, me_ref, g_ref, h_ref, wi_ref, wo_ref, out_ref, dh_ref, *grads):
    @pl.when(pl.program_id(0) == 0)
    def _():
        out_ref[...] = jnp.zeros_like(out_ref)
        dh_ref[...] = jnp.zeros_like(dh_ref)

    hidden = dot(h_ref[...], wi_ref[...], NN)
    back = dot(g_ref[...], wo_ref[...], NT)
    act, slope = gelu_pair(hidden)
    act = act.astype(BF16)
    out_ref[...] += dot(act, wo_ref[...], NN)
    low = (back * slope).astype(BF16)
    dh_ref[...] += dot(low, wi_ref[...], NT)
    even = me_ref[0] % 2 == 0
    if shares[0]:
        store_shares(dot(h_ref[...], low, TN), shares[0], even, *grads[:2])
    else:
        grads[0][...] = dot(h_ref[...], low, TN).astype(BF16)
    store_shares(dot(act, g_ref[...], TN), shares[1], even, *grads[-2:])


def mlp_both(grad, field, w_in, w_out, me, devices, tile):
    rows, wide = field.shape
    hidden = w_out.shape[0]
    whole = pl.BlockSpec((rows, wide), lambda i: (0, 0), pipeline_mode=pl.Buffered(1))
    total = pl.BlockSpec((rows, wide), lambda i: (0, 0))
    columns = pl.BlockSpec((wide, tile), lambda i: (0, i))
    in_rows, out_rows = (wide // devices, hidden // devices)
    in_specs = [pl.BlockSpec((devices // 2, in_rows, tile), lambda i: (0, 0, i))] * 2
    in_types = [share_type(devices, in_rows, hidden)] * 2
    if in_rows % 16:
        in_rows = 0
        in_specs = [columns]
        in_types = [jax.ShapeDtypeStruct((wide, hidden), BF16)]
    out_block = pl.BlockSpec((tile // out_rows // 2, out_rows, wide), lambda i: (i, 0, 0))
    outs = pl.pallas_call(
        functools.partial(mlp_both_kernel, (in_rows, out_rows)),
        grid=(hidden // tile,),
        in_specs=[SCALARS, whole, whole, columns, pl.BlockSpec((tile, wide), lambda i: (i, 0))],
        out_specs=[total, total] + in_specs + [out_block] * 2,
        out_shape=[
            jax.ShapeDtypeStruct((rows, wide), F32),
            jax.ShapeDtypeStruct((rows, wide), F32),
        ]
        + in_types
        + [share_type(devices, out_rows, wide)] * 2,
        compiler_params=kernel_limits(60),
        cost_estimate=estimate(14 * rows * wide * hidden, 8 * wide * hidden),
        name="mlp_both",
    )(me, grad, field, w_in, w_out)
    return (outs[0], outs[1], outs[2:-2], outs[-2:])


def expand_kernel(plan, tile, tiles, rows, me_ref, h_ref, *refs):
    sources = refs[: len(plan)]
    act_ref, slope_ref, natural, weights, sems = refs[len(plan) :]
    step = pl.program_id(0)
    me = me_ref[0]

    def load(number):
        slot = number % 2
        start_copies(
            plan, me, sources, weights.at[slot], sems.at[slot], number * tile, (number + 1) * tile
        )

    def save(number, slot):
        return pltpu.make_async_copy(
            weights.at[slot],
            natural.at[:, pl.ds(pl.multiple_of(number * tile, tile), tile)],
            sems.at[2 + slot],
        )

    @pl.when(step == 0)
    def _():
        load(0)

    slot = step % 2
    pltpu.make_async_copy(weights.at[slot], weights.at[slot], sems.at[slot]).wait()
    save(step, slot).start()

    @pl.when(step > 0)
    def _():
        save(step - 1, 1 - slot).wait()

    for number in range(1, tiles):

        @pl.when(step == number - 1)
        def _():
            load(number)

    def body(index, carry):
        spot = pl.ds(pl.multiple_of(index * rows, rows), rows)
        act, slope = gelu_pair(dot(h_ref[spot, :], weights[slot], NN))
        act_ref[spot, :] = act.astype(BF16)
        slope_ref[spot, :] = slope.astype(BF16)
        return carry

    lax.fori_loop(0, h_ref.shape[0] // rows, body, 0)

    @pl.when(step == tiles - 1)
    def _():
        save(step, slot).wait()


def expand(field, pieces, me, hidden, tile, step):
    plan, sources = pieces
    rows, wide = field.shape
    whole = pl.BlockSpec((rows, wide), lambda i: (0, 0), pipeline_mode=pl.Buffered(1))
    tiles = pl.BlockSpec((rows, tile), lambda i: (0, i))
    return pl.pallas_call(
        functools.partial(expand_kernel, plan, tile, hidden // tile, step),
        grid=(hidden // tile,),
        in_specs=[SCALARS, whole] + [ANYWHERE] * len(sources),
        out_specs=[tiles, tiles, ANYWHERE],
        out_shape=[
            jax.ShapeDtypeStruct((rows, hidden), BF16),
            jax.ShapeDtypeStruct((rows, hidden), BF16),
            jax.ShapeDtypeStruct((wide, hidden), BF16),
        ],
        scratch_shapes=[pltpu.VMEM((2, wide, tile), BF16), pltpu.SemaphoreType.DMA((4,))],
        compiler_params=kernel_limits(60),
        cost_estimate=estimate(4 * rows * wide * hidden, 4 * wide * hidden + 4 * rows * hidden),
        name="expand",
    )(me, field, *sources)


def shrink_kernel(plan, width, me_ref, live_ref, a_ref, x_ref, scale_ref, *refs):
    sources = refs[: len(plan)]
    out_ref, low_ref, next_ref, natural, weights, sems = refs[len(plan) :]
    live = live_ref[0].astype(F32)
    step = pl.program_id(0)
    parts = weights.shape[0]

    @pl.when(step == 0)
    def _():
        for place in range(parts):
            start_copies(
                plan,
                me_ref[0],
                sources,
                weights.at[place],
                sems.at[place],
                place * width,
                (place + 1) * width,
            )

    pltpu.make_async_copy(weights.at[step], weights.at[step], sems.at[step]).wait()
    save = pltpu.make_async_copy(
        weights.at[step],
        natural.at[:, pl.ds(pl.multiple_of(step * width, width), width)],
        sems.at[parts],
    )
    save.start()
    rows = 256

    def body(index, carry):
        spot = pl.ds(pl.multiple_of(index * rows, rows), rows)
        value = dot(a_ref[spot, :], weights[step], NN)
        out_ref[spot, :] = value
        hires = x_ref[spot, :].astype(F32) + scale_ref[...] * value
        low_ref[spot, :] = hires.astype(BF16)
        next_ref[spot, :] = (live * hires).astype(BF16)
        return carry

    lax.fori_loop(0, a_ref.shape[0] // rows, body, 0)
    save.wait()


def shrink(act, field, scale, live, pieces, me, width):
    plan, sources = pieces
    rows, hidden = act.shape
    columns = max(each[4] for each in plan)
    return pl.pallas_call(
        functools.partial(shrink_kernel, plan, width),
        grid=(columns // width,),
        in_specs=[
            SCALARS,
            SCALARS,
            pl.BlockSpec((rows, hidden), lambda i: (0, 0), pipeline_mode=pl.Buffered(1)),
            pl.BlockSpec((rows, width), lambda i: (0, i)),
            pl.BlockSpec((1, width), lambda i: (0, i)),
        ]
        + [ANYWHERE] * len(sources),
        out_specs=[pl.BlockSpec((rows, width), lambda i: (0, i))] * 3 + [ANYWHERE],
        out_shape=[
            jax.ShapeDtypeStruct((rows, columns), F32),
            jax.ShapeDtypeStruct((rows, columns), BF16),
            jax.ShapeDtypeStruct((rows, columns), BF16),
            jax.ShapeDtypeStruct((hidden, columns), BF16),
        ],
        scratch_shapes=[
            pltpu.VMEM((columns // width, hidden, width), BF16),
            pltpu.SemaphoreType.DMA((columns // width + 1,)),
        ],
        compiler_params=kernel_limits(60),
        cost_estimate=estimate(3 * rows * hidden * columns, 6 * hidden * columns),
        name="shrink",
    )(me, live, act, field, scale, *sources)


def outer_kernel(shares, me_ref, left_ref, right_ref, mine_ref, theirs_ref):
    value = dot(left_ref[...], right_ref[...], TN)
    store_shares(value, shares, me_ref[0] % 2 == 0, mine_ref, theirs_ref)


def outer_sum(left, right, me, share):
    rows, lines = left.shape
    columns = right.shape[1]
    if share % 16:
        return halves(dot(left, right, TN).astype(BF16).reshape(-1, share, columns), lines // share)
    tile = 4 * share if share >= 192 else 16 * share
    while lines % tile:
        tile //= 2
    block = pl.BlockSpec((tile // share // 2, share, columns), lambda i: (i, 0, 0))
    return pl.pallas_call(
        functools.partial(outer_kernel, share),
        grid=(lines // tile,),
        in_specs=[
            SCALARS,
            pl.BlockSpec((rows, tile), lambda i: (0, i)),
            pl.BlockSpec((rows, columns), lambda i: (0, 0), pipeline_mode=pl.Buffered(1)),
        ],
        out_specs=[block] * 2,
        out_shape=[share_type(lines // share, share, columns)] * 2,
        compiler_params=kernel_limits(48),
        cost_estimate=estimate(3 * rows * lines * columns, 2 * lines * columns),
        name="outer_sum",
    )(me, left, right)


def mlp_back_kernel(step, share, begun, me_ref, g_ref, h_ref, slope_ref, wi_ref, wo_ref, *refs):
    start_ref, dh_ref, *grads, low_ref = refs if begun else (None,) + refs

    @pl.when(pl.program_id(0) == 0)
    def _():
        dh_ref[...] = start_ref[...] if begun else jnp.zeros_like(dh_ref)

    def body(index, carry):
        spot = pl.ds(pl.multiple_of(index * step, step), step)
        back = dot(g_ref[spot, :], wo_ref[...], NT)
        low = (back * slope_ref[spot, :].astype(F32)).astype(BF16)
        low_ref[spot, :] = low
        dh_ref[spot, :] += dot(low, wi_ref[...], NT)
        return carry

    lax.fori_loop(0, h_ref.shape[0] // step, body, 0)
    block = h_ref.shape[1]
    even = me_ref[0] % 2 == 0

    def outer(index, carry):
        spot = pl.ds(pl.multiple_of(index * block, block), block)
        value = dot(h_ref[:, spot], low_ref[...], TN)
        if share:
            pairs = block // share // 2
            store_shares(value, share, even, *grads, pl.ds(index * pairs, pairs))
        else:
            grads[0][spot, :] = value.astype(BF16)
        return carry

    lax.fori_loop(0, h_ref.shape[1] // block, outer, 0)


def mlp_back(grad, field, slope, w_in, w_out, start, me, devices, tile, step, first, last):
    rows, wide = field.shape
    width = (last - first) * tile
    whole = pl.BlockSpec((rows, wide), lambda i: (0, 0), pipeline_mode=pl.Buffered(1))
    share = wide // devices
    grad_specs = [pl.BlockSpec((devices // 2, share, tile), lambda i: (0, 0, i))] * 2
    grad_types = [share_type(devices, share, width)] * 2
    if share % 16:
        share = 0
        grad_specs = [pl.BlockSpec((wide, tile), lambda i: (0, i))]
        grad_types = [jax.ShapeDtypeStruct((wide, width), BF16)]
    outs = pl.pallas_call(
        functools.partial(mlp_back_kernel, step, share, start is not None),
        grid=(last - first,),
        in_specs=[
            SCALARS,
            whole,
            whole,
            pl.BlockSpec((rows, tile), lambda i: (0, i + first)),
            pl.BlockSpec((wide, tile), lambda i: (0, i + first)),
            pl.BlockSpec((tile, wide), lambda i: (i + first, 0)),
        ]
        + ([] if start is None else [whole]),
        out_specs=[whole] + grad_specs,
        out_shape=[jax.ShapeDtypeStruct((rows, wide), F32)] + grad_types,
        scratch_shapes=[pltpu.VMEM((rows, tile), BF16)],
        compiler_params=kernel_limits(60),
        cost_estimate=estimate(7 * rows * wide * width, 6 * wide * width),
        name="mlp_back",
    )(me, grad, field, slope, w_in, w_out, *([] if start is None else [start]))
    return (outs[0], outs[1:])


def gate_kernel(share, me_ref, live_ref, mixed_ref, gv_ref, w_ref, gated_ref, dmix_ref, *grads):
    live = live_ref[0].astype(F32)
    mixed = mixed_ref[...]
    mixed_low = mixed.astype(BF16)
    wide = mixed.shape[1]
    wi, wo = (w_ref[:, :wide], w_ref[:, wide:])
    act, slope = gelu_pair(dot(mixed_low, wi, NN))
    act = act.astype(BF16)
    gate = jnp.tanh(dot(act, wo, NN))
    gated_ref[...] = gate * mixed
    grad = live * gv_ref[...].astype(F32)
    logit = (grad * mixed * (1.0 - gate * gate)).astype(BF16)
    low = (dot(logit, wo, NT) * slope).astype(BF16)
    for place, (left, right) in enumerate(((mixed_low, low), (act, logit))):
        lanes = slice(place * wide, (place + 1) * wide)
        if share:
            spot = (slice(None), slice(None), lanes)
            store_shares(dot(left, right, TN), share, me_ref[0] % 2 == 0, *grads, spot)
        else:
            grads[0][:, lanes] = dot(left, right, TN).astype(BF16)
    dmix_ref[...] = grad * gate + dot(low, wi, NT)


def gate_both(mixed, grad, live, me, weights, devices):
    rows, wide = mixed.shape
    share = wide // devices
    grad_types = [share_type(devices, share, 2 * wide)] * 2
    if share % 16:
        share = 0
        grad_types = [jax.ShapeDtypeStruct((wide, 2 * wide), BF16)]
    return pl.pallas_call(
        functools.partial(gate_kernel, share),
        in_specs=[SCALARS, SCALARS, LOCAL, LOCAL, LOCAL],
        out_specs=[LOCAL] * (2 + len(grad_types)),
        out_shape=[jax.ShapeDtypeStruct((rows, wide), F32)] * 2 + grad_types,
        compiler_params=kernel_limits(60),
        cost_estimate=estimate(20 * rows * wide * wide, 30 * rows * wide),
        name="gate_both",
    )(me, live, mixed, grad, weights)


def bit_pairs(devices, bit):
    return [(index, index ^ (1 << bit)) for index in range(devices)]


def own_bit(bit):
    return (lax.axis_index("fsdp") >> bit) & 1


def gather_small(block, devices):
    gathered = block[None]
    for bit in range(devices.bit_length() - 1):
        other = lax.ppermute(gathered, "fsdp", bit_pairs(devices, bit))
        high = own_bit(bit) == 1
        gathered = jnp.where(
            high,
            jnp.concatenate((other, gathered), axis=0),
            jnp.concatenate((gathered, other), axis=0),
        )
    return gathered


def after(values, earlier):
    if not earlier:
        return list(values)
    return list(lax.optimization_barrier(tuple(values) + tuple(earlier))[: len(values)])


def swap(block, bits, devices):
    mask = sum(1 << bit for bit in bits)
    return lax.ppermute(block, "fsdp", [(index, index ^ mask) for index in range(devices)])


def axis_bits(devices):
    bits = devices.bit_length() - 1
    if bits == 5:
        return ((1,), (2,), (3, 4))
    span = (bits - 1 + 2) // 3
    places = tuple(range(1, bits))
    return (places[:span], places[span : 2 * span], places[2 * span :])


def subsets(bits):
    found = [()]
    for bit in bits:
        found = found + [each + (bit,) for each in found]
    return found


def mask_of(bits):
    return sum(1 << bit for bit in bits)


class Gatherer:
    def __init__(self, devices):
        self.devices = devices
        self.x_bits, self.y_bits, self.z_bits = axis_bits(devices)
        self.last = []
        self.ends = []

    def doubled(self, field, slots, bits):
        for bit in bits:
            other = swap(field, (bit,), self.devices)
            field = jnp.concatenate((field, other), axis=0)
            slots = slots + [slot ^ (1 << bit) for slot in slots]
        return (field, slots)

    def group(self, block, begin, end, middle):
        rows = block.shape[0]
        (own,) = after((block[None, :, begin:end],), self.last)
        fields, slots = ([own], [0])
        for bits in subsets(self.z_bits)[1:]:
            fields.append(swap(own, bits, self.devices))
            slots.append(mask_of(bits))
        plan, sources, firsts, seconds = ([], [], [], [])
        for first, last, left, right in (
            (self.x_bits, self.y_bits, begin, middle),
            (self.y_bits, self.x_bits, middle, end),
        ):
            field = jnp.concatenate(
                [each[:, :, left - begin : right - begin] for each in fields], axis=0
            )
            (field,) = after((field,), self.ends)
            firsts.append((*self.doubled(field, slots, first), last, left, right))
        self.last = [each[0] for each in firsts]
        self.ends = []
        for field, its_slots, last, left, right in firsts:
            held = [(field, its_slots)]
            for bit in last + (0,):
                if bit == 0:
                    self.ends += [part for part, _ in held[1:]]
                held = held + [
                    (swap(part, (bit,), self.devices), [slot ^ (1 << bit) for slot in part_slots])
                    for part, part_slots in held
                ]
            for part, part_slots in held:
                sources.append(part)
                plan.append((tuple(part_slots), rows, 0, left, right))
        return (plan, sources)

    def weight(self, block, groups):
        plan, sources = ([], [])
        rows = block.shape[0]
        if rows % 16:
            whole = lax.all_gather(block, "fsdp", axis=0, tiled=True)[None]
            plan = [((None,), rows * self.devices, begin, begin, end) for begin, _, end in groups]
            return (plan, [whole] * len(groups))
        for begin, middle, end in groups:
            more_plan, more_sources = self.group(block, begin, end, middle)
            plan += more_plan
            sources += more_sources
        return (plan, sources)


def take(field, axis, place):
    return lax.dynamic_index_in_dim(field, place, axis, keepdims=False)


def halved(field, held, bit, devices):
    axis = held.index(bit)
    mine = own_bit(bit)
    arrived = swap(take(field, axis, 1 - mine), (bit,), devices)
    return (take(field, axis, mine) + arrived, held[:axis] + held[axis + 1 :])


def combine_kernel(parts, stacked, me_ref, *refs):
    count = 4 * sum(len(widths) for widths in parts)
    blocks, outs = (refs[:count], refs[count:])
    sums = []
    for widths in parts:
        kept, sent = ([], [])
        for _ in widths:
            (a, b, c, d), blocks = (blocks[:4], blocks[4:])
            kept.append((a[0].astype(F32) + b[0].astype(F32)).astype(BF16))
            sent.append((c[0].astype(F32) + d[0].astype(F32)).astype(BF16))
        sums.append((kept, sent))
    if not stacked:
        for place, pair in enumerate(sums):
            for out_ref, values in zip(outs[2 * place : 2 * place + 2], pair):
                begin = 0
                for value in values:
                    out_ref[0, :, begin : begin + value.shape[1]] = value
                    begin += value.shape[1]
        return
    for which, out_ref in enumerate(outs):
        line = 0
        for pair in sums:
            (value,) = pair[which]
            rows, columns = value.shape
            for begin in range(0, columns, stacked):
                out_ref[0, line : line + rows, :] = value[:, begin : begin + stacked]
                line += rows


def combine(me, parts, stacked):
    def spec(rows, width, bit, after_it, other, begin):
        def index(slot, me_ref):
            mine = (me_ref[0] >> bit) & 1
            mine = 1 - mine if other else mine
            return ((slot // after_it * 2 + mine) * after_it + slot % after_it, 0, begin // width)

        return pl.BlockSpec((1, rows, width), index)

    in_specs, operands, widths, shapes, moved = ([], [], [], [], 0)
    for bit, before, after_it, segments in parts:
        slots = before * after_it
        for kept, arrived, begin, width in segments:
            rows = kept.shape[1]
            for other in (False, True):
                in_specs += [spec(rows, width, bit, after_it, other, begin)] * 2
                operands += [kept, arrived]
            moved += 6 * slots * rows * width
        widths.append([segment[3] for segment in segments])
        shapes.append((rows, sum(widths[-1])))
    if stacked:
        total = sum(rows * columns // stacked for rows, columns in shapes)
        shapes = [(total, stacked)]
    out_specs, out_types = ([], [])
    for shape in shapes:
        out_specs += [pl.BlockSpec((1,) + shape, lambda slot, me_ref: (slot, 0, 0))] * 2
        out_types += [jax.ShapeDtypeStruct((slots,) + shape, BF16)] * 2
    outs = pl.pallas_call(
        functools.partial(combine_kernel, widths, stacked),
        grid_spec=pltpu.PrefetchScalarGridSpec(
            num_scalar_prefetch=1,
            grid=(slots,),
            in_specs=in_specs,
            out_specs=out_specs,
        ),
        out_shape=out_types,
        compiler_params=kernel_limits(48),
        cost_estimate=estimate(moved, 2 * moved),
        name="combine",
    )(me, *operands)
    return list(zip(outs[::2], outs[1::2]))


class Scatterer:
    def __init__(self, devices, me, gradients, parts, early=False):
        x_bits, y_bits, z_bits = axis_bits(devices)
        self.me = me
        self.bits = devices.bit_length() - 1
        self.orders = (y_bits + x_bits + z_bits, x_bits + y_bits + z_bits)
        self.split = 0 if early else len(x_bits + y_bits)
        if early:
            self.orders = (self.orders[0],) * 2
        self.parts = parts
        self.shapes = [
            (gradients[part[0][0]][0].shape[1], sum(width for _, _, width in part)) for part in parts
        ]
        self.width = min(columns for _, columns in self.shapes)
        self.stage = -1
        self.kept = [mine for mine, _ in gradients]
        self.sends = [(theirs, 0) for _, theirs in gradients]
        self.result = None

    def receive(self, arrived):
        pairs = list(zip(self.kept, arrived))
        self.stage += 1
        if self.stage == self.bits - 1:
            total = pairs[0][0][0].astype(F32) + pairs[0][1][0].astype(F32)
            self.sends, self.result = ([], [])
            line = 0
            for rows, columns in self.shapes:
                pieces = []
                for _ in range(columns // self.width):
                    pieces.append(total[line : line + rows])
                    line += rows
                self.result.append(jnp.concatenate(pieces, axis=1))
            return
        if self.stage == 0:
            segments = [
                [(*pairs[place], begin, width) for place, begin, width in part]
                for part in self.parts
            ]
            self.held = [list(range(self.bits - 1, 0, -1))] * 2
        else:
            segments = [[(*pair, 0, pair[0].shape[2])] for pair in pairs]
        parts, helds = ([], [])
        for order, held, its_segments in zip(self.orders, self.held, segments):
            bit = order[self.stage]
            axis = held.index(bit)
            parts.append((bit, 2**axis, 2 ** (len(held) - axis - 1), its_segments))
            helds.append(held[:axis] + held[axis + 1 :])
        self.held = helds
        sums = combine(self.me, parts, self.width if self.stage == self.split else 0)
        self.kept = [kept for kept, _ in sums]
        self.sends = [(sent, part[0]) for (_, sent), part in zip(sums, parts)]


class Ticks:
    def __init__(self):
        self.before = []

    def run(self, groups, value, work):
        groups = [group for group in groups if group.result is None]
        sends = [each for group in groups for each in group.sends]
        value, *blocks = after([value] + [block for block, _ in sends], self.before)
        devices = lax.axis_size("fsdp")
        arrived = [swap(block, (bit,), devices) for block, (_, bit) in zip(blocks, sends)]
        outs = jax.tree.leaves(work(value))
        done = after(outs + arrived, [])
        if len(done) > 1:
            done = list(lax.optimization_barrier(tuple(done)))
        outs, arrived = (done[: len(outs)], done[len(outs) :])
        begin = 0
        for group in groups:
            count = len(group.sends)
            group.receive(arrived[begin : begin + count])
            begin += count
        self.before = outs[:1]
        return outs

    def finish(self, groups):
        while any(group.result is None for group in groups):
            self.run(groups, jnp.zeros((), F32), lambda value: value)


def halves(gradient, devices):
    pairs = gradient.reshape((devices // 2, 2) + gradient.shape[1:])
    mine = own_bit(0)
    return (take(pairs, 1, mine), take(pairs, 1, 1 - mine))


def shards(
    x_vit,
    x_hires,
    image_live,
    grad_vit,
    grad_hires,
    gain_one,
    w_qkv,
    w_out,
    gain_two,
    w_up,
    w_down,
    conv_seven,
    gain_three,
    w_expand,
    w_shrink,
    layer_scale,
    w_adapt,
    conv_three,
    w_gate_in,
    w_gate_out,
):
    devices = lax.axis_size("fsdp")
    edge_c, edge_d = (gain_three.shape[0], gain_one.shape[0])
    small = jnp.concatenate(
        (
            conv_seven.reshape(-1),
            gain_three,
            layer_scale,
            conv_three.reshape(-1),
            gain_one,
            gain_two,
        )
    )
    small_all = gather_small(small, devices)
    marks = [0]
    for length in (KS * KS * edge_c, edge_c, edge_c, KA * KA * edge_d, edge_d, edge_d):
        marks.append(marks[-1] + length)
    small_parts = [small_all[:, marks[place] : marks[place + 1]] for place in range(6)]
    seven_taps = small_parts[0].reshape(devices, KS * KS, edge_c).swapaxes(0, 1).reshape(KS * KS, C)
    three_taps = small_parts[3].reshape(devices, KA * KA, edge_d).swapaxes(0, 1).reshape(KA * KA, D)
    gain_c, scale_c = (small_parts[1].reshape(C).astype(F32), small_parts[2].reshape(C).astype(F32))
    gain_a, gain_b = (small_parts[4].reshape(D).astype(F32), small_parts[5].reshape(D).astype(F32))

    me = lax.axis_index("fsdp").astype(jnp.int32).reshape(1)
    def gathered(block):
        return lax.all_gather(block, "fsdp", axis=0, tiled=True)

    live = image_live.astype(F32)
    vit_all = gathered(jnp.concatenate((w_qkv, w_out), axis=1))
    qkv_all, out_all = (vit_all[:, : 3 * D], vit_all[:, 3 * D :])
    gates_all = gathered(jnp.concatenate((w_gate_in, w_gate_out), axis=1))
    adapt_all = gathered(w_adapt)
    tile = D
    tiles = w_expand.shape[1] // tile
    gatherer = Gatherer(devices)
    expand_pieces = gatherer.weight(w_expand, [(0, C, 2 * C)])
    conved = depthwise(after((x_hires,), gatherer.last)[0], seven_taps, KS, GRID_HR)
    normed_c, inverse_c = norm_rows(conved, 1e-06)
    normed_c_low = (normed_c * gain_c).astype(BF16)
    gatherer.ends.append(normed_c_low)
    more_pieces = gatherer.weight(w_expand, [(2 * C, 3 * C, 4 * C)])
    expand_pieces = tuple(one + two for one, two in zip(expand_pieces, more_pieces))

    def attention(x_vit):
        patch_in = x_vit.astype(F32)
        normed_a, inverse_a = norm_rows(patch_in, 1e-05)
        normed_a_low = (normed_a * gain_a).astype(BF16)
        qkv_low = dot(normed_a_low, qkv_all, NN).astype(BF16)
        attended_low = attend(qkv_low)
        resid_one = patch_in + dot(attended_low, out_all, NN)
        normed_b, inverse_b = norm_rows(resid_one, 1e-05)
        normed_b_low = (normed_b * gain_b).astype(BF16)
        return (
            normed_b_low, qkv_low, attended_low, resid_one, normed_a, inverse_a, normed_b, inverse_b, normed_a_low
        )

    (
        normed_b_low, qkv_low, attended_low, resid_one, normed_a, inverse_a, normed_b, inverse_b, normed_a_low
    ) = attention(after((x_vit,), gatherer.last)[0])
    gatherer.ends.append(normed_b_low)
    shrink_pieces = gatherer.weight(w_shrink, [(0, C // 4, C // 2)])
    field_c = after((normed_c_low,), gatherer.last)[0]
    activated, slope, expand_all = expand(
        field_c, expand_pieces, me, w_expand.shape[1], tile, 256
    )
    gatherer.ends.append(activated)
    more_pieces = gatherer.weight(w_shrink, [(C // 2, 3 * C // 4, C)])
    shrink_pieces = tuple(one + two for one, two in zip(shrink_pieces, more_pieces))
    up_all = gathered(after((w_up,), gatherer.last)[0])
    down_all = gathered(after((w_down,), gatherer.last)[0])

    def shares(gradient):
        return gradient.reshape(devices, gradient.shape[0] // devices, gradient.shape[1])

    def split(gradient):
        if len(gradient) == 2:
            return tuple(gradient)
        return halves(shares(gradient[0]), devices)

    ticks = Ticks()

    shrunk, hires_low, hires_next, shrink_all = ticks.run(
        [],
        activated,
        lambda act: shrink(
            act, x_hires, scale_c.reshape(1, C), image_live, shrink_pieces, me, C // 2
        ),
    )

    pool = pool_matrix(GRID_HR, GRID_LR)

    def adapter(hires_low):
        pooled_low = dot(pool, hires_low, NN).astype(BF16)
        adapted = dot(pooled_low, adapt_all, NN)
        mixed = depthwise(adapted, three_taps, KA, GRID_LR)
        gated, grad_mixed, *d_gates = gate_both(
            mixed, grad_vit, image_live, me, gates_all, devices
        )
        return (grad_mixed, gated, pooled_low, adapted, *d_gates)

    grad_mixed, gated, pooled_low, adapted, *d_gates = ticks.run(
        [], hires_low, adapter
    )

    def adapter_back(grad_mixed):
        grad_adapted_low, d_conv_three = depthwise_back(
            grad_mixed, adapted, jnp.zeros(adapted.shape, BF16), three_taps, KA, GRID_LR, 0, D
        )
        d_adapt = outer_sum(pooled_low, grad_adapted_low, me, edge_c)
        grad_pooled_low = dot(grad_adapted_low, adapt_all, NT).astype(BF16)
        grad_hires_out = live * grad_hires.astype(F32) + dot(pool, grad_pooled_low, TN)
        d_layer_scale = jnp.sum(grad_hires_out * shrunk, axis=0)
        grad_shrunk_low = (grad_hires_out * scale_c).astype(BF16)
        return (grad_shrunk_low, d_layer_scale, grad_hires_out, d_conv_three, *d_adapt)

    grad_shrunk_low, d_layer_scale, grad_hires_out, d_conv_three, *d_adapt = ticks.run(
        [], grad_mixed, adapter_back
    )
    sum_square = Scatterer(
        devices,
        me,
        [split(d_gates), split(d_adapt)],
        [[(0, 0, 2 * D)], [(1, 0, D)]],
        early=True,
    )

    outs = ticks.run(
        [sum_square],
        grad_shrunk_low,
        lambda grad: outer_sum(activated, grad, me, w_shrink.shape[0]),
    )
    sum_shrink = Scatterer(
        devices, me, [tuple(outs)], [[(0, 0, C // 2)], [(0, C // 2, C // 2)]]
    )
    sums_expand = []

    def network_back(groups, grad_c, part):
        value = grad_shrunk_low if grad_c is None else grad_c
        sums, *d_part = ticks.run(
            groups,
            value,
            lambda value: mlp_back(
                value if grad_c is None else grad_shrunk_low,
                normed_c_low,
                slope,
                expand_all,
                shrink_all,
                None if grad_c is None else value,
                me,
                devices,
                tile,
                512,
                part * tiles // 2,
                (part + 1) * tiles // 2,
            ),
        )
        width = w_expand.shape[1] // 4
        sums_expand.append(
            Scatterer(devices, me, [split(d_part)], [[(0, 0, width)], [(0, width, width)]])
        )
        return sums

    grad_c = network_back([sum_square, sum_shrink], None, 0)

    grad_joined_low = (grad_vit.astype(F32) * live).astype(BF16)

    def network_both(field):
        mlp_out, grad_b, d_up, d_down = mlp_both(
            grad_joined_low, field, up_all, down_all, me, devices, D
        )
        return (mlp_out, grad_b, *d_up, *d_down)

    mlp_out, grad_b, *d_hidden = ticks.run(
        [sum_shrink, sums_expand[0]], normed_b_low, network_both
    )
    sum_mlp = Scatterer(
        devices,
        me,
        [split(d_hidden[:-2]), split(d_hidden[-2:])],
        [[(0, 0, w_up.shape[1])], [(1, 0, D)]],
    )
    joined = (live * (resid_one + mlp_out + gated)).astype(BF16)
    d_gain_two = jnp.sum(grad_b * normed_b, axis=0)
    grad_first = grad_joined_low.astype(F32) + norm_back(grad_b * gain_b, normed_b, inverse_b)
    grad_c = network_back([sum_shrink, sum_mlp, sum_square], grad_c, 1)

    def attention_back(grad_first):
        grad_first_low = grad_first.astype(BF16)
        grad_att_low = dot(grad_first_low, out_all, NT).astype(BF16)
        d_out = outer_sum(attended_low, grad_first_low, me, edge_d)
        return (*attend_back(qkv_low, grad_att_low), *d_out)

    *grads_three, out_mine, out_theirs = ticks.run(
        [sum_mlp, sum_shrink, sums_expand[1], sum_square], grad_first, attention_back
    )

    def projection_back(grad_queries):
        grad_qkv_low = jnp.concatenate((grad_queries, *grads_three[1:]), axis=1)
        d_qkv = outer_sum(normed_a_low, grad_qkv_low, me, edge_d)
        grad_a = dot(grad_qkv_low, qkv_all, NT)
        d_gain_one = jnp.sum(grad_a * normed_a, axis=0)
        grad_patches = grad_first + norm_back(grad_a * gain_a, normed_a, inverse_a)
        return (grad_patches, d_gain_one, *d_qkv)

    grad_patches, d_gain_one, *d_qkv = ticks.run(
        [sums_expand[0], sum_mlp, sum_shrink], grads_three[0], projection_back
    )
    sum_attention = Scatterer(
        devices,
        me,
        [tuple(d_qkv), (out_mine, out_theirs)],
        [[(0, 0, 2 * D)], [(0, 2 * D, D), (1, 0, D)]],
    )

    d_gain_three = jnp.sum(grad_c * normed_c, axis=0)
    grad_conved = norm_back(grad_c * gain_c, normed_c, inverse_c)
    grad_hires_in = grad_hires_out
    pieces_seven = []
    width = C // 3
    beside = (
        [sums_expand[1], sums_expand[0], sum_mlp],
        [sum_attention, sums_expand[1], sum_mlp],
        [sum_attention] + sums_expand,
    )
    for part in range(3):
        grad_hires_in, taps_part = ticks.run(
            beside[part],
            grad_hires_in,
            lambda base, part=part: depthwise_back(
                grad_conved,
                x_hires,
                base,
                seven_taps,
                KS,
                GRID_HR,
                part * width,
                (part + 1) * width,
            ),
        )
        pieces_seven.append(taps_part)
    d_conv_seven = jnp.concatenate(pieces_seven, axis=1)
    ticks.run([sum_attention, sum_square] + sums_expand, jnp.zeros((), F32), lambda value: value)
    small_grads = jnp.concatenate(
        (
            d_conv_seven.reshape(KS * KS, devices, edge_c).swapaxes(0, 1).reshape(devices, -1),
            d_gain_three.reshape(devices, edge_c),
            d_layer_scale.reshape(devices, edge_c),
            d_conv_three.reshape(KA * KA, devices, edge_d).swapaxes(0, 1).reshape(devices, -1),
            d_gain_one.reshape(devices, edge_d),
            d_gain_two.reshape(devices, edge_d),
        ),
        axis=1,
    )
    small_grads = after((small_grads,), ticks.before)[0]
    ticks.finish([sum_attention, sum_mlp, sum_shrink, sum_square] + sums_expand)
    g_up, g_down = sum_mlp.result
    g_attention = jnp.concatenate(sum_attention.result, axis=1)
    g_gates, g_adapt = sum_square.result
    g_shrink = jnp.concatenate(sum_shrink.result, axis=1)
    g_expand = jnp.concatenate([part for each in sums_expand for part in each.result], axis=1)
    small_sums = small_grads.reshape((2,) * (devices.bit_length() - 1) + small_grads.shape[1:])
    held = list(range(devices.bit_length() - 2, -1, -1))
    for bit in range(devices.bit_length() - 1):
        small_sums, held = halved(small_sums, held, bit, devices)
    small_outs = [small_sums[marks[place] : marks[place + 1]] for place in range(6)]
    return (
        joined,
        hires_next,
        grad_patches,
        grad_hires_in,
        small_outs[4],
        g_attention[:, : 3 * D],
        g_attention[:, 3 * D :],
        small_outs[5],
        g_up,
        g_down,
        small_outs[0].reshape(KS * KS, edge_c),
        small_outs[1],
        g_expand,
        g_shrink,
        small_outs[2],
        g_adapt,
        small_outs[3].reshape(KA * KA, edge_d),
        g_gates[:, :D],
        g_gates[:, D:],
    )


def solution(mesh):
    in_specs = (
        P("fsdp", None),
        P("fsdp", None),
        P("fsdp"),
        P("fsdp", None),
        P("fsdp", None),
        P("fsdp"),
        P("fsdp", None),
        P("fsdp", None),
        P("fsdp"),
        P("fsdp", None),
        P("fsdp", None),
        P(None, "fsdp"),
        P("fsdp"),
        P("fsdp", None),
        P("fsdp", None),
        P("fsdp"),
        P("fsdp", None),
        P(None, "fsdp"),
        P("fsdp", None),
        P("fsdp", None),
    )
    out_specs = (
        P("fsdp", None),
        P("fsdp", None),
        P("fsdp", None),
        P("fsdp", None),
        P("fsdp"),
        P("fsdp", None),
        P("fsdp", None),
        P("fsdp"),
        P("fsdp", None),
        P("fsdp", None),
        P(None, "fsdp"),
        P("fsdp"),
        P("fsdp", None),
        P("fsdp", None),
        P("fsdp"),
        P("fsdp", None),
        P(None, "fsdp"),
        P("fsdp", None),
        P("fsdp", None),
    )
    return jax.shard_map(shards, mesh=mesh, in_specs=in_specs, out_specs=out_specs, check_vma=False)
```
